32 devices in a mesh: blk: 4 (over y, x), dom: 8 (over z, core).
Axes of the slice: x: 2, y: 2, z: 4, core: 2. Of those that a mesh axis runs over, the one named last changes fastest.
Arguments:
- cell_features: bfloat16 [8, 1024, 768], P('dom', 'blk'), may hold values from -6 to 6
- cotangent: bfloat16 [8, 1024, 768], P('dom', 'blk'), may hold values from -6 to 6
- query_weight: bfloat16 [768, 768], replicated
- key_weight: bfloat16 [768, 768], replicated
- value_weight: bfloat16 [768, 768], replicated, may hold values from -0.21875 to 0.21875
- out_weight: bfloat16 [768, 768], replicated, may hold values from -0.21875 to 0.21875
- anchor_index: int32 [8, 128], P('dom', 'blk'), may hold values from 0 to 255, as said below
- face_cells: int32 [8, 4, 2, 128], P('dom', 'blk'), may hold values from 0 to 255, as said below
- halo_count: int32 [8, 4, 2], P('dom', 'blk'), may hold values from 0 to 128, as said below
- neighbour_blocks: int32 [8, 8, 3], P('dom', 'blk'), may hold values from 0 to 3, as said below
Outputs:
- mixed: bfloat16 [8, 1024, 768], P('dom', 'blk')
- cell_grad: bfloat16 [8, 1024, 768], P('dom', 'blk')
- weight_grads: float32 [3072, 768], P(('blk', 'dom'))
The draws below stay inside these ranges and needn't reach their ends.
Inputs may be any that keep to these rules, and one draw needn't show every extreme that they name: `anchor_index`: the 32 entries of one slot are different cells of that slot. `face_cells`: the 256 entries of one slot are different cells of that slot. halo_count[0, b, 0] and halo_count[7, b, 1] are 0 for every b; all other entries are 1 or more. `neighbour_blocks`: row b*2+j lists 3 different pool blocks, the first of them j itself.
All inputs are finite; a program needn't handle non-finite values.
Results may differ from the reference program's by a relative error of at most 0.017.
The reference program's roundings to bfloat16 on the way count: a program that leaves them out, or rounds other values in their place, can miss the bound.
Values may be sent and summed in bfloat16 or wider, within the bound.
A program may use at most 128 MiB of HBM per device.

```python
import math
import jax
import jax.numpy as jnp
from jax import lax

D = 768
HEADS = 12
BS = 128
NB = 3
C_DEV = 256
A_DEV = 32
QBLOCKS = 2
POOL = 4
PARTS_SIZE = 8
PART_CELLS = 1024
N_BLK = 4


def own_matrix(key):
    return jax.random.normal(key, (D, D), jnp.float32) / math.sqrt(D)


def draw_query_weight(key, part):
    key = jax.random.fold_in(key, 1)
    own = own_matrix(key)
    return own.astype(jnp.bfloat16)


def draw_key_weight(key, part):
    key = jax.random.fold_in(key, 2)
    own = own_matrix(key)
    return own.astype(jnp.bfloat16)


def slot_choice(key, amount):
    slot_keys = jax.random.split(key, PARTS_SIZE * N_BLK)

    def pick_slot(slot_key):
        return jax.random.permutation(slot_key, C_DEV)[:amount]
    return jax.vmap(pick_slot)(slot_keys).astype(jnp.int32)


def draw_anchor_index(key, part):
    key = jax.random.fold_in(key, 3)
    chosen = slot_choice(key, A_DEV)
    return chosen.reshape(PARTS_SIZE, N_BLK * A_DEV)


def draw_face_cells(key, part):
    key = jax.random.fold_in(key, 4)
    chosen = slot_choice(key, 2 * BS)
    return chosen.reshape(PARTS_SIZE, N_BLK, 2, BS)


def draw_halo_count(key, part):
    key = jax.random.fold_in(key, 5)
    drawn = jax.random.randint(key, (PARTS_SIZE, N_BLK, 2), 1, BS + 1)
    part_index = jnp.arange(PARTS_SIZE)[:, None, None]
    side = jnp.arange(2)[None, None, :]
    edge = (part_index == 0) & (side == 0) | (part_index == PARTS_SIZE - 1) & (side == 1)
    drawn = jnp.where(edge, 0, drawn)
    where_full = jax.random.randint(jax.random.fold_in(key, 9), (2,), 0, 1 << 20)
    full_part = 1 + where_full[0] % (PARTS_SIZE - 1)
    full_slot = where_full[1] % N_BLK
    drawn = drawn.at[full_part, full_slot, 0].set(BS)
    return drawn.astype(jnp.int32)


def draw_neighbour_blocks(key, part):
    key = jax.random.fold_in(key, 6)
    row_total = PARTS_SIZE * N_BLK * QBLOCKS
    raw = jax.random.randint(key, (row_total, POOL - 1), 0, 1 << 20)
    ranking = raw * POOL + jnp.arange(POOL - 1)[None, :]
    unused, picked = lax.top_k(ranking, NB - 1)
    itself = jnp.arange(row_total) % QBLOCKS
    others = (itself[:, None] + 1 + picked) % POOL
    table = jnp.concatenate([itself[:, None], others], 1).astype(jnp.int32)
    return table.reshape(PARTS_SIZE, N_BLK * QBLOCKS, NB)


def block_scale(stream_key, shape, pieces, least, largest):
    def one(dim, shards_of):
        heights = jax.random.uniform(jax.random.fold_in(jax.random.fold_in(stream_key, 6), dim), (shards_of,), jnp.float32, least / len(pieces), largest / len(pieces))
        return jnp.repeat(jnp.exp(heights), shape[dim] // shards_of).reshape((-1,) + (1,) * (len(shape) - dim - 1))

    factor_of = one(*pieces[0])
    for cut in pieces[1:]:
        factor_of = factor_of * one(*cut)
    return factor_of


def centred(rng, extent, deviation, most, cuts=(), kind=jnp.bfloat16):
    values = jax.random.normal(rng, extent, jnp.float32) * deviation
    if len(cuts) > 0:
        values = block_scale(rng, extent, cuts, -0.22, 0.18) * values
    return jnp.clip(values, min=-most, max=most).astype(kind)


def setup_inputs(seed: int = 0) -> dict:
    keys = jax.random.split(jax.random.key(seed), 11)
    cell_features = centred(keys[0], (PARTS_SIZE, PART_CELLS, D), 1.0, 6.0, ((0, 8), (1, 4)))
    cotangent = centred(keys[1], (PARTS_SIZE, PART_CELLS, D), 1.0, 6.0, ((0, 8), (1, 4)))
    query_weight = draw_query_weight(jax.random.fold_in(keys[10], 71), 0)
    key_weight = draw_key_weight(jax.random.fold_in(keys[10], 71), 0)
    value_weight = centred(keys[4], (D, D), D ** -0.5, 0.21875)
    out_weight = centred(keys[5], (D, D), D ** -0.5, 0.21875)
    anchor_index = draw_anchor_index(jax.random.fold_in(keys[10], 71), 0)
    face_cells = draw_face_cells(jax.random.fold_in(keys[10], 71), 0)
    halo_count = draw_halo_count(jax.random.fold_in(keys[10], 71), 0)
    neighbour_blocks = draw_neighbour_blocks(jax.random.fold_in(keys[10], 71), 0)
    return dict(cell_features=cell_features, cotangent=cotangent, query_weight=query_weight, key_weight=key_weight, value_weight=value_weight, out_weight=out_weight, anchor_index=anchor_index, face_cells=face_cells, halo_count=halo_count, neighbour_blocks=neighbour_blocks)


EPSILON = 1e-06
MASKED = -1e+30

def rounded(tensor):
    return lax.optimization_barrier(tensor.astype(jnp.bfloat16)).astype(jnp.float32)

def split_heads(tensor):
    leading = tensor.shape[:-2]
    length = tensor.shape[-2]
    tensor = tensor.reshape(leading + (length, HEADS, tensor.shape[-1] // HEADS))
    return jnp.moveaxis(tensor, -2, -3)

def join_heads(tensor):
    tensor = jnp.moveaxis(tensor, -3, -2)
    return tensor.reshape(tensor.shape[:-2] + (tensor.shape[-2] * tensor.shape[-1],))

def attend(queries, key_rows, value_rows, upstream, validity):
    scaling = 1.0 / math.sqrt(queries.shape[-1])
    q_float = queries.astype(jnp.float32)
    k_float = key_rows.astype(jnp.float32)
    v_float = value_rows.astype(jnp.float32)
    g_float = upstream.astype(jnp.float32)
    scores = jnp.einsum('...qe,...ke->...qk', q_float, k_float) * scaling
    scores = jnp.where(validity[..., None, :], scores, MASKED)
    highest = lax.optimization_barrier(jnp.max(scores, axis=-1, keepdims=True))
    powers = jnp.exp(scores - highest)
    probability = powers / lax.optimization_barrier(jnp.sum(powers, axis=-1, keepdims=True))
    prob_rounded = rounded(probability)
    out_rows = jnp.einsum('...qk,...ke->...qe', prob_rounded, v_float)
    prob_grad = jnp.einsum('...qe,...ke->...qk', g_float, v_float)
    score_grad = probability * (prob_grad - lax.optimization_barrier(jnp.sum(probability * prob_grad, axis=-1, keepdims=True)))
    score_rounded = rounded(score_grad)
    query_term = jnp.einsum('...qk,...ke->...qe', score_rounded, k_float) * scaling
    key_term = jnp.einsum('...qk,...qe->...ke', score_rounded, q_float) * scaling
    value_term = jnp.einsum('...qk,...qe->...ke', prob_rounded, g_float)
    return (out_rows, query_term, key_term, value_term)

def take_rows(table, index):
    return table[index]

def scatter_rows(base, index, addend):
    return base.at[index].add(addend)

def reference(cell_features, cotangent, query_weight, key_weight, value_weight, out_weight, anchor_index, face_cells, halo_count, neighbour_blocks):
    slot_count = PARTS_SIZE * N_BLK
    block_count = C_DEV // BS
    row_total = slot_count * C_DEV
    pick_rows = jax.vmap(take_rows)
    x_slot = cell_features.reshape(slot_count, C_DEV, D)
    dy_slot = cotangent.reshape(slot_count, C_DEV, D)
    as_float = x_slot.astype(jnp.float32)
    inverse = lax.rsqrt(lax.optimization_barrier(jnp.mean(as_float * as_float, axis=-1, keepdims=True)) + EPSILON)
    normed = (as_float * inverse).astype(jnp.bfloat16)
    flat = normed.reshape(row_total, D)

    def project(weight):
        return jnp.dot(flat, weight, preferred_element_type=jnp.float32).astype(jnp.bfloat16).reshape(slot_count, C_DEV, D)
    queries = project(query_weight)
    key_cells = project(key_weight)
    value_cells = project(value_weight)
    grad_mid = jnp.dot(dy_slot.reshape(row_total, D), out_weight.T, preferred_element_type=jnp.float32)
    grad_mid = grad_mid.astype(jnp.bfloat16).reshape(slot_count, C_DEV, D)
    anchor_rows = anchor_index.reshape(slot_count, A_DEV)
    anchor_keys = pick_rows(key_cells, anchor_rows).reshape(PARTS_SIZE, N_BLK * A_DEV, D)
    anchor_values = pick_rows(value_cells, anchor_rows).reshape(PARTS_SIZE, N_BLK * A_DEV, D)
    face_rows = face_cells.reshape(slot_count, 2 * BS)
    sent_keys = pick_rows(key_cells, face_rows).reshape(PARTS_SIZE, N_BLK, 2, BS, D)
    sent_values = pick_rows(value_cells, face_rows).reshape(PARTS_SIZE, N_BLK, 2, BS, D)
    zeros_block = jnp.zeros((1, N_BLK, BS, D), jnp.bfloat16)

    def pool_of(local, sent):
        lower = jnp.concatenate([zeros_block, sent[:-1, :, 1]], 0).reshape(slot_count, 1, BS, D)
        upper = jnp.concatenate([sent[1:, :, 0], zeros_block], 0).reshape(slot_count, 1, BS, D)
        return jnp.concatenate([local.reshape(slot_count, block_count, BS, D), lower, upper], 1)
    key_pool = pool_of(key_cells, sent_keys)
    value_pool = pool_of(value_cells, sent_values)
    live_count = halo_count.reshape(slot_count, 2)
    positions = jnp.arange(BS)
    live_rows = jnp.concatenate([jnp.ones((slot_count, block_count, BS), bool), (positions[None, :] < live_count[:, 0:1])[:, None], (positions[None, :] < live_count[:, 1:2])[:, None]], 1)
    near_index = neighbour_blocks.reshape(slot_count, block_count, NB)
    chosen_keys = pick_rows(key_pool, near_index)
    chosen_values = pick_rows(value_pool, near_index)
    chosen_live = pick_rows(live_rows, near_index)

    def by_part(tensor):
        return tensor.reshape((PARTS_SIZE, N_BLK) + tensor.shape[1:])

    def partition(members):
        q_part, g_part, keys_part, values_part, live_part, near_part, akey_part, aval_part = members
        akey_heads = split_heads(akey_part)
        aval_heads = split_heads(aval_part)
        all_live = jnp.ones((N_BLK * A_DEV,), bool)

        def slot_pass(totals, slot):
            q_slot, g_slot, keys_slot, values_slot, live_slot, near_slot = slot
            anchor_out, anchor_dquery, anchor_dkey, anchor_dvalue = attend(split_heads(q_slot), akey_heads, aval_heads, split_heads(g_slot), all_live)
            near_out, near_dquery, near_dkey, near_dvalue = attend(split_heads(q_slot.reshape(block_count, BS, D)), split_heads(keys_slot.reshape(block_count, NB * BS, D)), split_heads(values_slot.reshape(block_count, NB * BS, D)), split_heads(g_slot.reshape(block_count, BS, D)), live_slot.reshape(block_count, 1, NB * BS))
            attended = (join_heads(anchor_out) + join_heads(near_out).reshape(C_DEV, D)).astype(jnp.bfloat16)
            query_sum = join_heads(anchor_dquery) + join_heads(near_dquery).reshape(C_DEV, D)
            chosen_grad = jnp.concatenate([join_heads(near_dkey), join_heads(near_dvalue)], -1)
            chosen_grad = chosen_grad.reshape(block_count * NB, BS, 2 * D)
            pool_grad = jnp.zeros((block_count + 2, BS, 2 * D), jnp.float32).at[near_slot.reshape(-1)].add(chosen_grad)
            anchor_term = jnp.concatenate([join_heads(anchor_dkey), join_heads(anchor_dvalue)], -1)
            return (totals + rounded(anchor_term), (attended, query_sum, pool_grad))
        start = jnp.zeros((N_BLK * A_DEV, 2 * D), jnp.float32)
        anchor_grad, outputs = lax.scan(slot_pass, start, (q_part, g_part, keys_part, values_part, live_part, near_part))
        return outputs + (anchor_grad,)
    attended, query_sum, pool_grad, anchor_grad = lax.map(partition, (by_part(queries), by_part(grad_mid), by_part(chosen_keys), by_part(chosen_values), by_part(chosen_live), by_part(near_index), anchor_keys, anchor_values))
    attended = attended.reshape(slot_count, C_DEV, D)
    query_sum = query_sum.reshape(slot_count, C_DEV, D)
    pool_grad = pool_grad.reshape(slot_count, block_count + 2, BS, 2 * D)
    anchor_share = anchor_grad.reshape(slot_count, A_DEV, 2 * D)
    halo_grad = rounded(pool_grad[:, block_count:]).reshape(PARTS_SIZE, N_BLK, 2, BS, 2 * D)
    zeros_grad = jnp.zeros((1, N_BLK, BS, 2 * D), jnp.float32)
    to_lower = jnp.concatenate([zeros_grad, halo_grad[:-1, :, 1]], 0)
    to_upper = jnp.concatenate([halo_grad[1:, :, 0], zeros_grad], 0)
    came_back = jnp.stack([to_lower, to_upper], 2).reshape(slot_count, 2 * BS, 2 * D)
    keyval_grad = pool_grad[:, :block_count].reshape(slot_count, C_DEV, 2 * D)
    keyval_grad = jax.vmap(scatter_rows)(keyval_grad, anchor_rows, anchor_share)
    keyval_grad = jax.vmap(scatter_rows)(keyval_grad, face_rows, came_back)
    query_grad = query_sum.astype(jnp.bfloat16)
    key_grad = keyval_grad[..., :D].astype(jnp.bfloat16)
    value_grad = keyval_grad[..., D:].astype(jnp.bfloat16)

    def outer_sum(left, right):
        return jnp.dot(left.reshape(row_total, D).T, right.reshape(row_total, D), preferred_element_type=jnp.float32)
    weight_grads = jnp.concatenate([outer_sum(normed, query_grad), outer_sum(normed, key_grad), outer_sum(normed, value_grad), outer_sum(attended, dy_slot)], 0)

    def back_project(grad_rows, weight):
        return jnp.dot(grad_rows.reshape(row_total, D), weight.T, preferred_element_type=jnp.float32).reshape(slot_count, C_DEV, D)
    normed_grad = back_project(query_grad, query_weight) + back_project(key_grad, key_weight) + back_project(value_grad, value_weight)
    cot_float = dy_slot.astype(jnp.float32)
    cube = inverse * inverse * inverse
    cell_grad = cot_float + inverse * normed_grad - as_float * cube * lax.optimization_barrier(jnp.mean(normed_grad * as_float, axis=-1, keepdims=True))
    mixed = as_float + jnp.dot(attended.reshape(row_total, D), out_weight, preferred_element_type=jnp.float32).reshape(slot_count, C_DEV, D)
    mixed = mixed.astype(jnp.bfloat16).reshape(PARTS_SIZE, N_BLK * C_DEV, D)
    cell_grad = cell_grad.astype(jnp.bfloat16).reshape(PARTS_SIZE, N_BLK * C_DEV, D)
    return (mixed, cell_grad, weight_grads)
```

```python
import functools

import jax
import jax.numpy as jnp
from jax import lax
from jax.experimental import pallas as pl
from jax.experimental.pallas import tpu as pltpu
from jax.sharding import PartitionSpec as P

HEAD = 64
PAIR = 2 * HEAD
BS = 128
EPSILON = 1e-06
MASKED = -1e30
SCALING = 0.125
MESH = pl.DeviceIdType.MESH
F32 = jnp.float32
BF16 = jnp.bfloat16


def mm(a, b):
    return lax.dot_general(a, b, (((1,), (0,)), ((), ())), preferred_element_type=F32)


def mm_nt(a, b):
    return lax.dot_general(a, b, (((1,), (1,)), ((), ())), preferred_element_type=F32)


def mm_tn(a, b):
    return lax.dot_general(a, b, (((0,), (0,)), ((), ())), preferred_element_type=F32)


def attend(q2, g2, keys, values, live):
    scores = mm_nt(q2, keys)
    if live is not None:
        scores = jnp.where(jnp.broadcast_to(live, scores.shape) > 0, scores, MASKED)
    powers = jnp.exp(scores - jnp.max(scores, axis=-1, keepdims=True))
    prob = powers * (1.0 / jnp.sum(powers, axis=-1, keepdims=True))
    prob_b = prob.astype(BF16)
    out = mm(prob_b, values)
    prob_grad = mm_nt(g2, values)
    score_grad = prob * (prob_grad - jnp.sum(prob * prob_grad, axis=-1, keepdims=True))
    score_b = score_grad.astype(BF16)
    query_term = mm(score_b, keys) * SCALING
    key_term = mm_tn(score_b, q2)
    value_term = mm_tn(prob_b, g2)
    return out, query_term, key_term, value_term


def kernel(
    n_blk,
    n_dom,
    x_ref,
    dy_ref,
    wq_ref,
    wk_ref,
    wv_ref,
    wo_ref,
    idx_ref,
    count_ref,
    near_ref,
    mixed_ref,
    cgrad_ref,
    wgrad_ref,
    normed,
    q_s,
    g_s,
    kv_s,
    hot_s,
    faces,
    anchors,
    halo,
    ag_out,
    ag_in,
    hg_out,
    hg_in,
    near_s,
    att_f,
    qg_f,
    att_b,
    grads,
    lhs,
    rhs,
    wsum,
    wpart,
    from_left,
    from_right,
    anc_send,
    anc_recv,
    face_send,
    face_recv,
    lhs_send,
    lhs_recv,
    rhs_send,
    rhs_recv,
    ag_send,
    ag_recv,
    hg_send,
    hg_recv,
    core_sem,
    right_send,
    right_recv,
    left_send,
    left_recv,
):
    cells, width = x_ref.shape
    rows = lhs.shape[2]
    share = wsum.shape[2]
    chips = n_dom // 2
    pairs = width // PAIR
    blk = lax.axis_index("blk")
    dom = lax.axis_index("dom")
    chip = dom // 2
    core = dom - 2 * chip
    mate = dom + 1 - 2 * core

    def copy(src, dst, send, recv, target):
        return pltpu.make_async_remote_copy(
            src_ref=src,
            dst_ref=dst,
            send_sem=send,
            recv_sem=recv,
            device_id=target,
            device_id_type=MESH,
        )

    def each_peer(action):
        for j in range(n_blk):
            pl.when(blk != j)(functools.partial(action, j))

    barrier = pltpu.get_barrier_semaphore()
    steps = (-2, -1, 1, 2)

    def greet(target):
        pl.semaphore_signal(barrier, inc=1, device_id=target, device_id_type=MESH)

    each_peer(lambda j: greet({"blk": j}))
    for step in steps:
        there = (dom + step >= 0) & (dom + step < n_dom)
        pl.when(there)(functools.partial(lambda s: greet({"dom": dom + s}), step))

    x = x_ref[...].astype(F32)
    inverse = lax.rsqrt(jnp.mean(x * x, axis=-1, keepdims=True) + EPSILON)
    normed[...] = (x * inverse).astype(BF16)
    kv_s[:, :width] = mm(normed[...], wk_ref[...]).astype(BF16)
    kv_s[:, width:] = mm(normed[...], wv_ref[...]).astype(BF16)

    spots = lax.broadcasted_iota(jnp.int32, hot_s.shape, 0)
    hot_s[...] = jnp.where(spots == idx_ref[...], 1.0, 0.0).astype(BF16)
    picked = 2 * BS + anchors.shape[1]
    for part in range(2):
        columns = slice(part * width, (part + 1) * width)
        chosen = mm_tn(hot_s[:, : 3 * BS], kv_s[:, columns]).astype(BF16)
        faces[0, :, columns] = chosen[:BS]
        faces[1, :, columns] = chosen[BS : 2 * BS]
        anchors[blk, :, columns] = chosen[2 * BS : picked]

    expected = n_blk - 1
    for step in steps:
        there = (dom + step >= 0) & (dom + step < n_dom)
        expected = expected + jnp.where(there, 1, 0)
    pl.semaphore_wait(barrier, expected)

    has_low = dom > 0
    has_high = dom < n_dom - 1

    def anchor_copy(j):
        return copy(
            anchors.at[blk], anchors.at[blk], anc_send.at[j], anc_recv.at[blk], {"blk": j}
        )

    def anchor_arrival(j):
        return copy(anchors.at[j], anchors.at[j], anc_send.at[j], anc_recv.at[j], {"blk": j})

    def face_copy(side):
        step = 2 * side - 1
        return copy(
            faces.at[side],
            halo.at[1 - side],
            face_send.at[side],
            face_recv.at[1 - side],
            {"dom": dom + step},
        )

    def weight_of(j):
        return (j * rows) // width, (j * rows) % width

    def lhs_copy(j):
        weight, start = weight_of(j)
        source = normed if weight < 3 else att_b
        return copy(
            source.at[:, start : start + rows],
            lhs.at[blk],
            lhs_send.at[j],
            lhs_recv.at[blk],
            {"blk": j},
        )

    def rhs_copy(j):
        weight, _ = weight_of(j)
        source = grads.at[weight] if weight < 3 else dy_ref
        return copy(source, rhs.at[blk], rhs_send.at[j], rhs_recv.at[blk], {"blk": j})

    def lhs_own(j):
        weight, start = weight_of(j)
        source = normed if weight < 3 else att_b
        lhs[j] = source[:, start : start + rows]

    def rhs_own(j):
        weight, _ = weight_of(j)
        rhs[j] = grads[weight] if weight < 3 else dy_ref[...]

    def send_lhs(wanted):
        for j in range(n_blk):
            if weight_of(j)[0] in wanted:
                pl.when(blk != j)(functools.partial(lambda k: lhs_copy(k).start(), j))
                pl.when(blk == j)(functools.partial(lhs_own, j))

    def send_rhs(wanted):
        for j in range(n_blk):
            if weight_of(j)[0] in wanted:
                pl.when(blk != j)(functools.partial(lambda k: rhs_copy(k).start(), j))
                pl.when(blk == j)(functools.partial(rhs_own, j))

    each_peer(lambda j: anchor_copy(j).start())
    pl.when(has_low)(lambda: face_copy(0).start())
    pl.when(has_high)(lambda: face_copy(1).start())
    send_lhs((0, 1, 2))
    send_rhs((3,))

    q_s[...] = mm(normed[...], wq_ref[...]).astype(BF16)
    g_s[...] = mm_nt(dy_ref[...], wo_ref[...]).astype(BF16)

    @pl.when(jnp.logical_not(has_low))
    def _():
        halo[0] = jnp.zeros(halo.shape[1:], BF16)
        hg_in[0] = jnp.zeros(hg_in.shape[1:], BF16)

    @pl.when(jnp.logical_not(has_high))
    def _():
        halo[1] = jnp.zeros(halo.shape[1:], BF16)
        hg_in[1] = jnp.zeros(hg_in.shape[1:], BF16)

    lane = lax.broadcasted_iota(jnp.int32, (1, PAIR), 1)
    first = jnp.where(lane < HEAD, 1.0, 0.0)
    first_b = first.astype(BF16)
    second_b = (1.0 - first).astype(BF16)

    def stacked(rows_of, scale):
        return jnp.concatenate([rows_of * (first_b * scale), rows_of * (second_b * scale)], 0)

    def unstacked(tensor):
        half = tensor.shape[0] // 2
        keep = jnp.broadcast_to(first, (half, PAIR)) > 0
        return jnp.where(keep, tensor[:half], tensor[half:])

    each_peer(lambda j: anchor_arrival(j).wait_recv())
    anchor_count = n_blk * anchors.shape[1]

    def anchor_pair(h, carry):
        sl = pl.ds(pl.multiple_of(h * PAIR, PAIR), PAIR)
        vsl = pl.ds(pl.multiple_of(width + h * PAIR, PAIR), PAIR)
        q2 = stacked(q_s[:, sl], SCALING)
        g2 = stacked(g_s[:, sl], 1.0)
        keys = anchors[:, :, sl].reshape(anchor_count, PAIR)
        values = anchors[:, :, vsl].reshape(anchor_count, PAIR)
        out, query_term, key_term, value_term = attend(q2, g2, keys, values, None)
        att_f[:, sl] = unstacked(out)
        qg_f[:, sl] = unstacked(query_term)
        ag_out[:, :, sl] = key_term.astype(BF16).reshape(n_blk, -1, PAIR)
        ag_out[:, :, vsl] = value_term.astype(BF16).reshape(n_blk, -1, PAIR)
        return carry

    lax.fori_loop(0, pairs, anchor_pair, 0)

    def ag_copy(j):
        return copy(ag_out.at[j], ag_in.at[blk], ag_send.at[j], ag_recv.at[blk], {"blk": j})

    def ag_arrival(j):
        return copy(ag_out.at[j], ag_in.at[j], ag_send.at[j], ag_recv.at[j], {"blk": j})

    each_peer(lambda j: ag_copy(j).start())
    ag_in[blk] = ag_out[blk]

    def face_arrival(side):
        step = 2 * side - 1
        return copy(
            faces.at[side],
            halo.at[side],
            face_send.at[side],
            face_recv.at[side],
            {"dom": dom + step},
        )

    pl.when(has_low)(lambda: face_arrival(0).wait_recv())
    pl.when(has_high)(lambda: face_arrival(1).wait_recv())

    blocks = cells // BS
    pool_rows = cells + 2 * BS
    spot = lax.broadcasted_iota(jnp.int32, (1, pool_rows), 1)
    zero = jnp.zeros((1, pool_rows), jnp.int32)
    one = zero + 1
    live_to = jnp.where(
        spot < cells, pool_rows, jnp.where(spot < cells + BS, cells, cells + BS)
    )
    live_to = live_to + jnp.where(
        spot < cells,
        0,
        jnp.where(spot < cells + BS, zero + count_ref[0, 0], zero + count_ref[0, 1]),
    )
    alive = jnp.where(spot < live_to, one, zero)
    live = []
    for j in range(blocks):
        listed = zero
        for i in range(near_ref.shape[1]):
            low = near_ref[j, i] * BS
            inside = jnp.where(spot >= low, one, zero) * jnp.where(spot < low + BS, one, zero)
            listed = listed + inside
        live.append((listed * alive).astype(F32))

    def near_pair(h, carry):
        sl = pl.ds(pl.multiple_of(h * PAIR, PAIR), PAIR)
        vsl = pl.ds(pl.multiple_of(width + h * PAIR, PAIR), PAIR)
        keys = jnp.concatenate([kv_s[:, sl], halo[0, :, sl], halo[1, :, sl]], 0)
        values = jnp.concatenate([kv_s[:, vsl], halo[0, :, vsl], halo[1, :, vsl]], 0)
        key_sum = value_sum = None
        for j in range(blocks):
            own = slice(j * BS, (j + 1) * BS)
            q2 = stacked(q_s[own, sl], SCALING)
            g2 = stacked(g_s[own, sl], 1.0)
            out, query_term, key_term, value_term = attend(q2, g2, keys, values, live[j])
            att_f[own, sl] += unstacked(out)
            qg_f[own, sl] += unstacked(query_term)
            key_sum = key_term if key_sum is None else key_sum + key_term
            value_sum = value_term if value_sum is None else value_sum + value_term
        near_s[:, sl] = key_sum[:cells]
        near_s[:, vsl] = value_sum[:cells]
        for side in range(2):
            part = slice(cells + side * BS, cells + (side + 1) * BS)
            hg_out[side, :, sl] = key_sum[part].astype(BF16)
            hg_out[side, :, vsl] = value_sum[part].astype(BF16)
        return carry

    lax.fori_loop(0, pairs, near_pair, 0)

    def hg_copy(side):
        step = 2 * side - 1
        return copy(
            hg_out.at[side],
            hg_in.at[1 - side],
            hg_send.at[side],
            hg_recv.at[1 - side],
            {"dom": dom + step},
        )

    def hg_arrival(side):
        step = 2 * side - 1
        return copy(
            hg_out.at[side],
            hg_in.at[side],
            hg_send.at[side],
            hg_recv.at[side],
            {"dom": dom + step},
        )

    pl.when(has_low)(lambda: hg_copy(0).start())
    pl.when(has_high)(lambda: hg_copy(1).start())
    att_b[...] = att_f[...].astype(BF16)
    grads[0] = qg_f[...].astype(BF16)
    send_lhs((3,))
    send_rhs((0,))

    each_peer(lambda j: ag_arrival(j).wait_recv())
    pl.when(has_low)(lambda: hg_arrival(0).wait_recv())
    pl.when(has_high)(lambda: hg_arrival(1).wait_recv())

    for part in (0, 1):
        columns = slice(part * width, (part + 1) * width)
        came = jnp.concatenate(
            [
                hg_in[0, :, columns],
                hg_in[1, :, columns],
                ag_in[:, :, columns].reshape(anchor_count, width),
            ],
            0,
        )
        grads[1 + part] = (near_s[:, columns] + mm(hot_s[...], came)).astype(BF16)
        send_rhs((1 + part,))

    mixed_ref[...] = (x_ref[...].astype(F32) + mm(att_b[...], wo_ref[...])).astype(BF16)
    back = mm_nt(grads[0], wq_ref[...]) + mm_nt(grads[1], wk_ref[...])
    back = back + mm_nt(grads[2], wv_ref[...])
    x = x_ref[...].astype(F32)
    inverse = lax.rsqrt(jnp.mean(x * x, axis=-1, keepdims=True) + EPSILON)
    cube = inverse * inverse * inverse
    pull = jnp.mean(back * x, axis=-1, keepdims=True)
    cgrad_ref[...] = (dy_ref[...].astype(F32) + inverse * back - x * (cube * pull)).astype(BF16)

    def operand_arrivals(j):
        copy(lhs.at[j], lhs.at[j], lhs_send.at[j], lhs_recv.at[j], {"blk": j}).wait_recv()
        copy(rhs.at[j], rhs.at[j], rhs_send.at[j], rhs_recv.at[j], {"blk": j}).wait_recv()

    each_peer(operand_arrivals)
    left_all = lhs[...].reshape(n_blk * cells, rows)
    right_all = rhs[...].reshape(n_blk * cells, width)
    product = mm_tn(left_all, right_all)
    for d in range(n_dom):
        wsum[d % 2, d // 2] = product[d * share : (d + 1) * share]

    swap = copy(wsum.at[1 - core], wpart, core_sem.at[0], core_sem.at[1], {"dom": mate})
    swap.start()
    swap.wait_recv()
    wsum[core] += wpart[...]

    def right_copy(source, t):
        return copy(
            source, from_left.at[t], right_send.at[t], right_recv.at[t], {"dom": dom + 2}
        )

    def left_copy(source, t):
        return copy(
            source, from_right.at[t], left_send.at[t], left_recv.at[t], {"dom": dom - 2}
        )

    def right_arrival(t):
        return copy(
            from_left.at[t], from_left.at[t], right_send.at[t], right_recv.at[t], {"dom": dom - 2}
        )

    def left_arrival(t):
        return copy(
            from_right.at[t], from_right.at[t], left_send.at[t], left_recv.at[t], {"dom": dom + 2}
        )

    last = chips - 1
    for step in range(chips - 1):
        t_right = last - step + chip
        t_left = step - (last - chip)

        @pl.when(chip == 0)
        def _():
            right_copy(wsum.at[core, t_right], t_right).start()

        @pl.when((chip > 0) & (chip <= step))
        def _():
            right_arrival(t_right).wait_recv()
            from_left[t_right] += wsum[core, t_right]
            right_copy(from_left.at[t_right], t_right).start()

        @pl.when(chip == last)
        def _():
            left_copy(wsum.at[core, t_left], t_left).start()

        @pl.when((chip < last) & (last - chip <= step))
        def _():
            left_arrival(t_left).wait_recv()
            from_right[t_left] += wsum[core, t_left]
            left_copy(from_right.at[t_left], t_left).start()

    wgrad_ref[...] = wsum[core, chip]

    @pl.when(chip > 0)
    def _():
        right_arrival(chip).wait_recv()
        wgrad_ref[...] += from_left[chip]

    @pl.when(chip < last)
    def _():
        left_arrival(chip).wait_recv()
        wgrad_ref[...] += from_right[chip]

    each_peer(lambda j: anchor_copy(j).wait_send())
    each_peer(lambda j: ag_copy(j).wait_send())
    each_peer(lambda j: lhs_copy(j).wait_send())
    each_peer(lambda j: rhs_copy(j).wait_send())

    @pl.when(has_low)
    def _():
        face_copy(0).wait_send()
        hg_copy(0).wait_send()

    @pl.when(has_high)
    def _():
        face_copy(1).wait_send()
        hg_copy(1).wait_send()

    swap.wait_send()
    for step in range(chips - 1):
        t_right = last - step + chip
        t_left = step - (last - chip)

        @pl.when(chip <= step)
        def _():
            right_copy(from_left.at[t_right], t_right).wait_send()

        @pl.when(last - chip <= step)
        def _():
            left_copy(from_right.at[t_left], t_left).wait_send()


def body(
    cell_features,
    cotangent,
    query_weight,
    key_weight,
    value_weight,
    out_weight,
    anchor_index,
    face_cells,
    halo_count,
    neighbour_blocks,
):
    n_blk = lax.axis_size("blk")
    n_dom = lax.axis_size("dom")
    _, cells, width = cell_features.shape
    own_anchors = anchor_index.shape[1]
    rows = 4 * width // n_blk
    share = rows // n_dom
    chips = n_dom // 2
    picks = jnp.concatenate(
        [face_cells.reshape(1, 2 * BS)] + [anchor_index] * n_blk, axis=1
    )
    vmem = pl.BlockSpec(memory_space=pltpu.VMEM)
    smem = pl.BlockSpec(memory_space=pltpu.SMEM)
    dma = pltpu.SemaphoreType.DMA
    peers = [dma((n_blk,)) for _ in range(2)]
    sides = [dma((2,)) for _ in range(2)]
    mixed, cell_grad, weight_grads = pl.pallas_call(
        functools.partial(kernel, n_blk, n_dom),
        out_shape=(
            jax.ShapeDtypeStruct((cells, width), BF16),
            jax.ShapeDtypeStruct((cells, width), BF16),
            jax.ShapeDtypeStruct((share, width), F32),
        ),
        in_specs=[vmem] * 7 + [smem] * 2,
        out_specs=(vmem, vmem, vmem),
        scratch_shapes=[
            pltpu.VMEM((cells, width), BF16),
            pltpu.VMEM((cells, width), BF16),
            pltpu.VMEM((cells, width), BF16),
            pltpu.VMEM((cells, 2 * width), BF16),
            pltpu.VMEM((cells, 2 * BS + n_blk * own_anchors), BF16),
            pltpu.VMEM((2, BS, 2 * width), BF16),
            pltpu.VMEM((n_blk, own_anchors, 2 * width), BF16),
            pltpu.VMEM((2, BS, 2 * width), BF16),
            pltpu.VMEM((n_blk, own_anchors, 2 * width), BF16),
            pltpu.VMEM((n_blk, own_anchors, 2 * width), BF16),
            pltpu.VMEM((2, BS, 2 * width), BF16),
            pltpu.VMEM((2, BS, 2 * width), BF16),
            pltpu.VMEM((cells, 2 * width), F32),
            pltpu.VMEM((cells, width), F32),
            pltpu.VMEM((cells, width), F32),
            pltpu.VMEM((cells, width), BF16),
            pltpu.VMEM((3, cells, width), BF16),
            pltpu.VMEM((n_blk, cells, rows), BF16),
            pltpu.VMEM((n_blk, cells, width), BF16),
            pltpu.VMEM((2, chips, share, width), F32),
            pltpu.VMEM((chips, share, width), F32),
            pltpu.VMEM((chips, share, width), F32),
            pltpu.VMEM((chips, share, width), F32),
            *peers,
            *sides,
            *peers,
            *peers,
            *peers,
            *sides,
            dma((2,)),
            *[dma((chips,)) for _ in range(4)],
        ],
        compiler_params=pltpu.CompilerParams(
            collective_id=0, has_side_effects=True, vmem_limit_bytes=56 * 1024 * 1024
        ),
    )(
        cell_features[0],
        cotangent[0],
        query_weight,
        key_weight,
        value_weight,
        out_weight,
        picks,
        halo_count.reshape(1, 2),
        neighbour_blocks[0],
    )
    return mixed[None], cell_grad[None], weight_grads


def solution(mesh):
    return jax.shard_map(
        body,
        mesh=mesh,
        in_specs=(
            P("dom", "blk", None),
            P("dom", "blk", None),
            P(),
            P(),
            P(),
            P(),
            P("dom", "blk"),
            P("dom", "blk", None, None),
            P("dom", "blk", None),
            P("dom", "blk", None),
        ),
        out_specs=(P("dom", "blk", None), P("dom", "blk", None), P(("blk", "dom"), None)),
        check_vma=False,
    )
```

```python
import functools

import jax
import jax.numpy as jnp
from jax import lax
from jax.experimental import pallas as pl
from jax.experimental.pallas import tpu as pltpu
from jax.sharding import PartitionSpec as P

HEAD = 64
PAIR = 2 * HEAD
BS = 128
EPSILON = 1e-06
MASKED = -1e30
LAG = 2
PIECES = 3
SCALING = 0.125
MESH = pl.DeviceIdType.MESH
F32 = jnp.float32
BF16 = jnp.bfloat16


def mm(a, b):
    return lax.dot_general(a, b, (((1,), (0,)), ((), ())), preferred_element_type=F32)


def mm_nt(a, b):
    return lax.dot_general(a, b, (((1,), (1,)), ((), ())), preferred_element_type=F32)


def mm_tn(a, b):
    return lax.dot_general(a, b, (((0,), (0,)), ((), ())), preferred_element_type=F32)


def attend(q2, g2, keys, values, live):
    scores = mm_nt(q2, keys)
    if live is not None:
        scores = jnp.where(jnp.broadcast_to(live, scores.shape) > 0, scores, MASKED)
    powers = jnp.exp(scores - jnp.max(scores, axis=-1, keepdims=True))
    prob = powers * (1.0 / jnp.sum(powers, axis=-1, keepdims=True))
    prob_b = prob.astype(BF16)
    out = mm(prob_b, values)
    prob_grad = mm_nt(g2, values)
    score_grad = prob * (prob_grad - jnp.sum(prob * prob_grad, axis=-1, keepdims=True))
    score_b = score_grad.astype(BF16)
    query_term = mm(score_b, keys) * SCALING
    key_term = mm_tn(score_b, q2)
    value_term = mm_tn(prob_b, g2)
    return out, query_term, key_term, value_term


def kernel(
    n_blk,
    n_dom,
    x_ref,
    dy_ref,
    wq_ref,
    wk_ref,
    wv_ref,
    wo_ref,
    anchor_ref,
    face_ref,
    count_ref,
    near_ref,
    mixed_ref,
    cgrad_ref,
    wgrad_ref,
    normed,
    q_s,
    g_s,
    kv_s,
    hot_s,
    faces,
    anchors,
    halo,
    ag_out,
    ag_in,
    hg_out,
    hg_in,
    near_s,
    att_f,
    qg_f,
    att_b,
    grads,
    lhs,
    rhs,
    wsum,
    wpart,
    from_left,
    from_right,
    anc_send,
    anc_recv,
    face_send,
    face_recv,
    early_send,
    early_recv,
    late_send,
    late_recv,
    ag_send,
    ag_recv,
    hg_send,
    hg_recv,
    core_send,
    core_recv,
    right_send,
    right_recv,
    left_send,
    left_recv,
):
    cells, width = x_ref.shape
    rows = lhs.shape[2]
    share = wsum.shape[3]
    piece = wsum.shape[4]
    chips = n_dom // 2
    pairs = width // PAIR
    blk = lax.axis_index("blk")
    dom = lax.axis_index("dom")
    chip = dom // 2
    core = dom - 2 * chip
    mate = dom + 1 - 2 * core

    def copy(src, dst, send, recv, target):
        return pltpu.make_async_remote_copy(
            src_ref=src,
            dst_ref=dst,
            send_sem=send,
            recv_sem=recv,
            device_id=target,
            device_id_type=MESH,
        )

    def each_peer(action):
        for j in range(n_blk):
            pl.when(blk != j)(functools.partial(action, j))

    barrier = pltpu.get_barrier_semaphore()
    steps = (-2, -1, 1, 2)

    def greet(target):
        pl.semaphore_signal(barrier, inc=1, device_id=target, device_id_type=MESH)

    each_peer(lambda j: greet({"blk": j}))
    for step in steps:
        there = (dom + step >= 0) & (dom + step < n_dom)
        pl.when(there)(functools.partial(lambda s: greet({"dom": dom + s}), step))

    x = x_ref[...].astype(F32)
    inverse = lax.rsqrt(jnp.mean(x * x, axis=-1, keepdims=True) + EPSILON)
    normed[...] = (x * inverse).astype(BF16)
    kv_s[:, :width] = mm(normed[...], wk_ref[...]).astype(BF16)
    kv_s[:, width:] = mm(normed[...], wv_ref[...]).astype(BF16)

    own_anchors = anchors.shape[1]
    anchor_count = n_blk * own_anchors
    spots = lax.broadcasted_iota(jnp.int32, (cells, BS), 0)
    for side in range(2):
        hits = jnp.where(spots == face_ref[side : side + 1, :], 1.0, 0.0)
        hot_s[:, side * BS : (side + 1) * BS] = hits.astype(BF16)
    turn = lax.broadcasted_iota(jnp.int32, (own_anchors, anchor_count), 1) % own_anchors
    same = lax.broadcasted_iota(jnp.int32, (own_anchors, anchor_count), 0) == turn
    listed = jnp.broadcast_to(anchor_ref[...].astype(F32), (8, own_anchors)).astype(BF16)
    repeated = mm(listed, jnp.where(same, 1.0, 0.0).astype(BF16))[:1]
    places = lax.broadcasted_iota(jnp.int32, (cells, anchor_count), 0).astype(F32)
    hot_s[:, 2 * BS :] = jnp.where(places == repeated, 1.0, 0.0).astype(BF16)
    picked = 2 * BS + anchors.shape[1]
    for part in range(2):
        columns = slice(part * width, (part + 1) * width)
        chosen = mm_tn(hot_s[:, : 3 * BS], kv_s[:, columns]).astype(BF16)
        faces[0, :, columns] = chosen[:BS]
        faces[1, :, columns] = chosen[BS : 2 * BS]
        anchors[blk, :, columns] = chosen[2 * BS : picked]

    expected = n_blk - 1
    for step in steps:
        there = (dom + step >= 0) & (dom + step < n_dom)
        expected = expected + jnp.where(there, 1, 0)
    pl.semaphore_wait(barrier, expected)

    has_low = dom > 0
    has_high = dom < n_dom - 1

    def anchor_copy(j):
        return copy(
            anchors.at[blk], anchors.at[blk], anc_send.at[j], anc_recv.at[blk], {"blk": j}
        )

    def anchor_arrival(j):
        return copy(anchors.at[j], anchors.at[j], anc_send.at[j], anc_recv.at[j], {"blk": j})

    def face_copy(side):
        step = 2 * side - 1
        return copy(
            faces.at[side],
            halo.at[1 - side],
            face_send.at[side],
            face_recv.at[1 - side],
            {"dom": dom + step},
        )

    def weight_of(j):
        return (j * rows) // width, (j * rows) % width

    def early_copy(j):
        weight, start = weight_of(j)
        if weight < 3:
            source, target = normed.at[:, start : start + rows], lhs.at[blk]
        else:
            source, target = dy_ref, rhs.at[blk]
        return copy(source, target, early_send.at[j], early_recv.at[blk], {"blk": j})

    def early_own(j):
        weight, start = weight_of(j)
        if weight < 3:
            lhs[j] = normed[:, start : start + rows]
        else:
            rhs[j] = dy_ref[...]

    def strip(h):
        return pl.ds(pl.multiple_of(h * PAIR, PAIR), PAIR)

    def late_copy(j, h):
        weight, start = weight_of(j)
        to = h - start // PAIR if weight == 3 else h
        source = grads.at[weight, :, strip(h)] if weight < 3 else att_b.at[:, strip(h)]
        target = rhs.at[blk, :, strip(to)] if weight < 3 else lhs.at[blk, :, strip(to)]
        return copy(source, target, late_send.at[j, to], late_recv.at[blk, to], {"blk": j})

    def send_late(weight, h):
        for j in range(n_blk):
            this, start = weight_of(j)
            if this != weight:
                continue

            def send(j=j):
                late_copy(j, h).start()

            def own(j=j, start=start):
                if weight < 3:
                    rhs[j, :, strip(h)] = grads[weight, :, strip(h)]
                else:
                    lhs[j, :, strip(h - start // PAIR)] = att_b[:, strip(h)]

            wanted = True
            if weight == 3 and rows < width:
                wanted = (h >= start // PAIR) & (h < (start + rows) // PAIR)
            pl.when((blk != j) & wanted)(send)
            pl.when((blk == j) & wanted)(own)

    def send_early(j):
        pl.when(blk != j)(lambda: early_copy(j).start())
        pl.when(blk == j)(lambda: early_own(j))

    each_peer(lambda j: anchor_copy(j).start())
    pl.when(has_low)(lambda: face_copy(0).start())
    pl.when(has_high)(lambda: face_copy(1).start())
    for j in range(n_blk):
        send_early(j)

    q_s[...] = mm(normed[...], wq_ref[...]).astype(BF16)
    g_s[...] = mm_nt(dy_ref[...], wo_ref[...]).astype(BF16)

    @pl.when(jnp.logical_not(has_low))
    def _():
        halo[0] = jnp.zeros(halo.shape[1:], BF16)
        hg_in[0] = jnp.zeros(hg_in.shape[1:], BF16)

    @pl.when(jnp.logical_not(has_high))
    def _():
        halo[1] = jnp.zeros(halo.shape[1:], BF16)
        hg_in[1] = jnp.zeros(hg_in.shape[1:], BF16)

    lane = lax.broadcasted_iota(jnp.int32, (1, PAIR), 1)
    first = jnp.where(lane < HEAD, 1.0, 0.0)
    first_b = first.astype(BF16)
    second_b = (1.0 - first).astype(BF16)

    def stacked(rows_of, scale):
        return jnp.concatenate([rows_of * (first_b * scale), rows_of * (second_b * scale)], 0)

    def unstacked(tensor):
        half = tensor.shape[0] // 2
        keep = jnp.broadcast_to(first, (half, PAIR)) > 0
        return jnp.where(keep, tensor[:half], tensor[half:])

    each_peer(lambda j: anchor_arrival(j).wait_recv())
    def anchor_pair(h, carry):
        sl = pl.ds(pl.multiple_of(h * PAIR, PAIR), PAIR)
        vsl = pl.ds(pl.multiple_of(width + h * PAIR, PAIR), PAIR)
        q2 = stacked(q_s[:, sl], SCALING)
        g2 = stacked(g_s[:, sl], 1.0)
        keys = anchors[:, :, sl].reshape(anchor_count, PAIR)
        values = anchors[:, :, vsl].reshape(anchor_count, PAIR)
        out, query_term, key_term, value_term = attend(q2, g2, keys, values, None)
        att_f[:, sl] = unstacked(out)
        qg_f[:, sl] = unstacked(query_term)
        ag_out[:, :, sl] = key_term.astype(BF16).reshape(n_blk, -1, PAIR)
        ag_out[:, :, vsl] = value_term.astype(BF16).reshape(n_blk, -1, PAIR)
        return carry

    lax.fori_loop(0, pairs, anchor_pair, 0)

    def ag_copy(j):
        return copy(ag_out.at[j], ag_in.at[blk], ag_send.at[j], ag_recv.at[blk], {"blk": j})

    def ag_arrival(j):
        return copy(ag_out.at[j], ag_in.at[j], ag_send.at[j], ag_recv.at[j], {"blk": j})

    each_peer(lambda j: ag_copy(j).start())
    ag_in[blk] = ag_out[blk]

    def face_arrival(side):
        step = 2 * side - 1
        return copy(
            faces.at[side],
            halo.at[side],
            face_send.at[side],
            face_recv.at[side],
            {"dom": dom + step},
        )

    pl.when(has_low)(lambda: face_arrival(0).wait_recv())
    pl.when(has_high)(lambda: face_arrival(1).wait_recv())

    blocks = cells // BS
    pool_rows = cells + 2 * BS
    spot = lax.broadcasted_iota(jnp.int32, (1, pool_rows), 1)
    zero = jnp.zeros((1, pool_rows), jnp.int32)
    one = zero + 1
    live_to = jnp.where(
        spot < cells, pool_rows, jnp.where(spot < cells + BS, cells, cells + BS)
    )
    live_to = live_to + jnp.where(
        spot < cells,
        0,
        jnp.where(spot < cells + BS, zero + count_ref[0, 0], zero + count_ref[0, 1]),
    )
    alive = jnp.where(spot < live_to, one, zero)
    live = []
    for j in range(blocks):
        listed = zero
        for i in range(near_ref.shape[1]):
            low = near_ref[j, i] * BS
            inside = jnp.where(spot >= low, one, zero) * jnp.where(spot < low + BS, one, zero)
            listed = listed + inside
        live.append((listed * alive).astype(F32))

    def hg_copy(side, h):
        step = 2 * side - 1
        return copy(
            hg_out.at[side, h],
            hg_in.at[1 - side, h],
            hg_send.at[side, h],
            hg_recv.at[1 - side, h],
            {"dom": dom + step},
        )

    def hg_arrival(side, h):
        step = 2 * side - 1
        return copy(
            hg_out.at[side, h],
            hg_in.at[side, h],
            hg_send.at[side, h],
            hg_recv.at[side, h],
            {"dom": dom + step},
        )

    def finish(h):
        pl.when(has_low)(lambda: hg_arrival(0, h).wait_recv())
        pl.when(has_high)(lambda: hg_arrival(1, h).wait_recv())
        sl = strip(h)
        vsl = pl.ds(pl.multiple_of(width + h * PAIR, PAIR), PAIR)
        shares = jnp.concatenate([ag_in[:, :, sl], ag_in[:, :, vsl]], -1)
        came = jnp.concatenate(
            [hg_in[0, h], hg_in[1, h], shares.reshape(anchor_count, 2 * PAIR)], 0
        )
        total = near_s[h] + mm(hot_s[...], came)
        grads[1, :, sl] = total[:, :PAIR].astype(BF16)
        grads[2, :, sl] = total[:, PAIR:].astype(BF16)
        send_late(1, h)
        send_late(2, h)

    def near_pair(h, carry):
        sl = pl.ds(pl.multiple_of(h * PAIR, PAIR), PAIR)
        vsl = pl.ds(pl.multiple_of(width + h * PAIR, PAIR), PAIR)
        keys = jnp.concatenate([kv_s[:, sl], halo[0, :, sl], halo[1, :, sl]], 0)
        values = jnp.concatenate([kv_s[:, vsl], halo[0, :, vsl], halo[1, :, vsl]], 0)
        key_sum = value_sum = None
        for j in range(blocks):
            own = slice(j * BS, (j + 1) * BS)
            q2 = stacked(q_s[own, sl], SCALING)
            g2 = stacked(g_s[own, sl], 1.0)
            out, query_term, key_term, value_term = attend(q2, g2, keys, values, live[j])
            att_b[own, sl] = (att_f[own, sl] + unstacked(out)).astype(BF16)
            grads[0, own, sl] = (qg_f[own, sl] + unstacked(query_term)).astype(BF16)
            key_sum = key_term if key_sum is None else key_sum + key_term
            value_sum = value_term if value_sum is None else value_sum + value_term
        near_s[h, :, :PAIR] = key_sum[:cells]
        near_s[h, :, PAIR:] = value_sum[:cells]
        for side in range(2):
            part = slice(cells + side * BS, cells + (side + 1) * BS)
            hg_out[side, h, :, :PAIR] = key_sum[part].astype(BF16)
            hg_out[side, h, :, PAIR:] = value_sum[part].astype(BF16)
        pl.when(has_low)(lambda: hg_copy(0, h).start())
        pl.when(has_high)(lambda: hg_copy(1, h).start())
        send_late(3, h)
        send_late(0, h)

        @pl.when(h == LAG)
        def _():
            each_peer(lambda j: ag_arrival(j).wait_recv())

        @pl.when(h >= LAG)
        def _():
            finish(h - LAG)

        return carry

    lax.fori_loop(0, pairs, near_pair, 0)

    def last_pair(h, carry):
        finish(h)
        return carry

    lax.fori_loop(pairs - LAG, pairs, last_pair, 0)

    is_out = blk * rows >= 3 * width

    def late_arrival(j, h, buffer):
        ref = buffer.at[j, :, strip(h)]
        return copy(ref, ref, late_send.at[j, h], late_recv.at[j, h], {"blk": j})

    def early_arrival(j, buffer):
        ref = buffer.at[j]
        return copy(ref, ref, early_send.at[j], early_recv.at[j], {"blk": j})

    def arrivals(first_buffer, second_buffer, count, j):
        early_arrival(j, first_buffer).wait_recv()

        def one(h, carry):
            late_arrival(j, h, second_buffer).wait_recv()
            return carry

        lax.fori_loop(0, count, one, 0)

    @pl.when(is_out)
    def _():
        each_peer(functools.partial(arrivals, rhs, lhs, rows // PAIR))

    @pl.when(jnp.logical_not(is_out))
    def _():
        each_peer(functools.partial(arrivals, lhs, rhs, pairs))

    def swap(n):
        return copy(
            wsum.at[n, 1 - core], wpart.at[n], core_send.at[n], core_recv.at[n], {"dom": mate}
        )

    left_all = lhs[...].reshape(n_blk * cells, rows)
    for n in range(PIECES):
        columns = slice(n * piece, (n + 1) * piece)
        product = mm_tn(left_all, rhs[:, :, columns].reshape(n_blk * cells, piece))
        for d in range(n_dom):
            wsum[n, d % 2, d // 2] = product[d * share : (d + 1) * share]
        swap(n).start()

    def right_copy(source, n, t):
        return copy(
            source.at[n, t],
            from_left.at[n, t],
            right_send.at[n, t],
            right_recv.at[n, t],
            {"dom": dom + 2},
        )

    def left_copy(source, n, t):
        return copy(
            source.at[n, t],
            from_right.at[n, t],
            left_send.at[n, t],
            left_recv.at[n, t],
            {"dom": dom - 2},
        )

    def right_arrival(n, t):
        ref = from_left.at[n, t]
        return copy(ref, ref, right_send.at[n, t], right_recv.at[n, t], {"dom": dom - 2})

    def left_arrival(n, t):
        ref = from_right.at[n, t]
        return copy(ref, ref, left_send.at[n, t], left_recv.at[n, t], {"dom": dom + 2})

    last = chips - 1
    for step in range(chips - 1):
        t_right = last - step + chip
        t_left = step - (last - chip)
        for n in range(PIECES):
            if step == 0:
                swap(n).wait_recv()
                wpart[n] += wsum[n, core]

            @pl.when(chip == 0)
            def _():
                right_copy(wpart, n, t_right).start()

            @pl.when((chip > 0) & (chip <= step))
            def _():
                right_arrival(n, t_right).wait_recv()
                from_left[n, t_right] += wpart[n, t_right]
                right_copy(from_left, n, t_right).start()

            @pl.when(chip == last)
            def _():
                left_copy(wpart, n, t_left).start()

            @pl.when((chip < last) & (last - chip <= step))
            def _():
                left_arrival(n, t_left).wait_recv()
                from_right[n, t_left] += wpart[n, t_left]
                left_copy(from_right, n, t_left).start()

        if step > 0:
            continue
        mixed_ref[...] = (x_ref[...].astype(F32) + mm(att_b[...], wo_ref[...])).astype(BF16)
        back = mm_nt(grads[0], wq_ref[...]) + mm_nt(grads[1], wk_ref[...])
        back = back + mm_nt(grads[2], wv_ref[...])
        x = x_ref[...].astype(F32)
        inverse = lax.rsqrt(jnp.mean(x * x, axis=-1, keepdims=True) + EPSILON)
        cube = inverse * inverse * inverse
        pull = jnp.mean(back * x, axis=-1, keepdims=True)
        cgrad_ref[...] = (dy_ref[...].astype(F32) + inverse * back - x * (cube * pull)).astype(BF16)

    for n in range(PIECES):
        columns = slice(n * piece, (n + 1) * piece)
        wgrad_ref[:, columns] = wpart[n, chip]

        @pl.when(chip > 0)
        def _():
            right_arrival(n, chip).wait_recv()
            wgrad_ref[:, columns] += from_left[n, chip]

        @pl.when(chip < last)
        def _():
            left_arrival(n, chip).wait_recv()
            wgrad_ref[:, columns] += from_right[n, chip]

    each_peer(lambda j: anchor_copy(j).wait_send())
    each_peer(lambda j: ag_copy(j).wait_send())
    each_peer(lambda j: early_copy(j).wait_send())

    def late_sent(j):
        weight, start = weight_of(j)
        low, high = (0, pairs) if weight < 3 else (start // PAIR, (start + rows) // PAIR)

        def one(h, carry):
            late_copy(j, h).wait_send()
            return carry

        lax.fori_loop(low, high, one, 0)

    each_peer(late_sent)

    def hg_sent(side):
        face_copy(side).wait_send()

        def one(h, carry):
            hg_copy(side, h).wait_send()
            return carry

        lax.fori_loop(0, pairs, one, 0)

    pl.when(has_low)(lambda: hg_sent(0))
    pl.when(has_high)(lambda: hg_sent(1))
    for n in range(PIECES):
        swap(n).wait_send()
        for step in range(chips - 1):
            t_right = last - step + chip
            t_left = step - (last - chip)

            @pl.when(chip <= step)
            def _():
                right_copy(from_left, n, t_right).wait_send()

            @pl.when(last - chip <= step)
            def _():
                left_copy(from_right, n, t_left).wait_send()


def deliver(*refs):
    count = len(refs) // 3
    sources, targets, sems = refs[:count], refs[count : 2 * count], refs[2 * count :]
    copies = [pltpu.make_async_copy(*each) for each in zip(sources, targets, sems)]
    for each in copies:
        each.start()
    for each in copies:
        each.wait()


def body(
    cell_features,
    cotangent,
    query_weight,
    key_weight,
    value_weight,
    out_weight,
    anchor_index,
    face_cells,
    halo_count,
    neighbour_blocks,
):
    n_blk = lax.axis_size("blk")
    n_dom = lax.axis_size("dom")
    _, cells, width = cell_features.shape
    own_anchors = anchor_index.shape[1]
    rows = 4 * width // n_blk
    share = rows // n_dom
    chips = n_dom // 2
    piece = width // PIECES
    pairs = width // PAIR
    vmem = pl.BlockSpec(memory_space=pltpu.VMEM)
    smem = pl.BlockSpec(memory_space=pltpu.SMEM)
    dma = pltpu.SemaphoreType.DMA
    peers = [dma((n_blk,)) for _ in range(2)]
    sides = [dma((2,)) for _ in range(2)]
    chain = dma((PIECES, chips))
    mixed, cell_grad, weight_grads = pl.pallas_call(
        functools.partial(kernel, n_blk, n_dom),
        out_shape=(
            jax.ShapeDtypeStruct((cells, width), BF16),
            jax.ShapeDtypeStruct((cells, width), BF16),
            jax.ShapeDtypeStruct((share, width), F32),
        ),
        in_specs=[vmem] * 8 + [smem] * 2,
        out_specs=(vmem, vmem, vmem),
        scratch_shapes=[
            pltpu.VMEM((cells, width), BF16),
            pltpu.VMEM((cells, width), BF16),
            pltpu.VMEM((cells, width), BF16),
            pltpu.VMEM((cells, 2 * width), BF16),
            pltpu.VMEM((cells, 2 * BS + n_blk * own_anchors), BF16),
            pltpu.VMEM((2, BS, 2 * width), BF16),
            pltpu.VMEM((n_blk, own_anchors, 2 * width), BF16),
            pltpu.VMEM((2, BS, 2 * width), BF16),
            pltpu.VMEM((n_blk, own_anchors, 2 * width), BF16),
            pltpu.VMEM((n_blk, own_anchors, 2 * width), BF16),
            pltpu.VMEM((2, pairs, BS, 2 * PAIR), BF16),
            pltpu.VMEM((2, pairs, BS, 2 * PAIR), BF16),
            pltpu.VMEM((pairs, cells, 2 * PAIR), F32),
            pltpu.VMEM((cells, width), F32),
            pltpu.VMEM((cells, width), F32),
            pltpu.VMEM((cells, width), BF16),
            pltpu.VMEM((3, cells, width), BF16),
            pltpu.VMEM((n_blk, cells, rows), BF16),
            pltpu.VMEM((n_blk, cells, width), BF16),
            pltpu.VMEM((PIECES, 2, chips, share, piece), F32),
            pltpu.VMEM((PIECES, chips, share, piece), F32),
            pltpu.VMEM((PIECES, chips, share, piece), F32),
            pltpu.VMEM((PIECES, chips, share, piece), F32),
            *peers,
            *sides,
            *peers,
            dma((n_blk, pairs)),
            dma((n_blk, pairs)),
            *peers,
            dma((2, pairs)),
            dma((2, pairs)),
            dma((PIECES,)),
            dma((PIECES,)),
            chain,
            chain,
            chain,
            chain,
        ],
        compiler_params=pltpu.CompilerParams(
            collective_id=0, has_side_effects=True, vmem_limit_bytes=56 * 1024 * 1024
        ),
    )(
        cell_features[0],
        cotangent[0],
        query_weight,
        key_weight,
        value_weight,
        out_weight,
        anchor_index,
        face_cells.reshape(2, BS),
        halo_count.reshape(1, 2),
        neighbour_blocks[0],
    )
    anywhere = pl.BlockSpec(memory_space=pl.ANY)
    results = (mixed, cell_grad, weight_grads)
    mixed, cell_grad, weight_grads = pl.pallas_call(
        deliver,
        out_shape=tuple(jax.ShapeDtypeStruct(each.shape, each.dtype) for each in results),
        in_specs=[anywhere] * 3,
        out_specs=(anywhere,) * 3,
        scratch_shapes=[dma, dma, dma],
    )(*results)
    return mixed[None], cell_grad[None], weight_grads


def solution(mesh):
    return jax.shard_map(
        body,
        mesh=mesh,
        in_specs=(
            P("dom", "blk", None),
            P("dom", "blk", None),
            P(),
            P(),
            P(),
            P(),
            P("dom", "blk"),
            P("dom", "blk", None, None),
            P("dom", "blk", None),
            P("dom", "blk", None),
        ),
        out_specs=(P("dom", "blk", None), P("dom", "blk", None), P(("blk", "dom"), None)),
        check_vma=False,
    )
```

```python
import functools

import jax
import jax.numpy as jnp
from jax import lax
from jax.experimental import pallas as pl
from jax.experimental.pallas import tpu as pltpu
from jax.sharding import PartitionSpec as P

HEAD = 64
PAIR = 2 * HEAD
BS = 128
EPSILON = 1e-06
MASKED = -1e30
LAG = 2
PIECES = 3
SCALING = 0.125
MESH = pl.DeviceIdType.MESH
F32 = jnp.float32
BF16 = jnp.bfloat16


def mm(a, b):
    return lax.dot_general(a, b, (((1,), (0,)), ((), ())), preferred_element_type=F32)


def mm_nt(a, b):
    return lax.dot_general(a, b, (((1,), (1,)), ((), ())), preferred_element_type=F32)


def mm_tn(a, b):
    return lax.dot_general(a, b, (((0,), (0,)), ((), ())), preferred_element_type=F32)


def attend(q2, g2, keys, values, live):
    scores = mm_nt(q2, keys)
    if live is not None:
        scores = jnp.where(jnp.broadcast_to(live, scores.shape) > 0, scores, MASKED)
    powers = jnp.exp(scores - jnp.max(scores, axis=-1, keepdims=True))
    prob = powers * (1.0 / jnp.sum(powers, axis=-1, keepdims=True))
    prob_b = prob.astype(BF16)
    out = mm(prob_b, values)
    prob_grad = mm_nt(g2, values)
    score_grad = prob * (prob_grad - jnp.sum(prob * prob_grad, axis=-1, keepdims=True))
    score_b = score_grad.astype(BF16)
    query_term = mm(score_b, keys) * SCALING
    key_term = mm_tn(score_b, q2)
    value_term = mm_tn(prob_b, g2)
    return out, query_term, key_term, value_term


def kernel(
    n_blk,
    n_dom,
    x_ref,
    dy_ref,
    wq_ref,
    wk_ref,
    wv_ref,
    wo_ref,
    anchor_ref,
    face_ref,
    count_ref,
    near_ref,
    mixed_ref,
    cgrad_ref,
    wgrad_ref,
    normed,
    q_s,
    g_s,
    kv_s,
    hot_s,
    faces,
    anchors,
    halo,
    ag_out,
    ag_in,
    hg_out,
    hg_in,
    near_s,
    att_f,
    qg_f,
    att_b,
    grads,
    lhs,
    rhs,
    lhs_t,
    wsum,
    wpart,
    from_left,
    from_right,
    anc_send,
    anc_recv,
    face_send,
    face_recv,
    early_send,
    early_recv,
    late_send,
    late_recv,
    ag_send,
    ag_recv,
    hg_send,
    hg_recv,
    core_send,
    core_recv,
    right_send,
    right_recv,
    left_send,
    left_recv,
):
    cells, width = x_ref.shape
    rows = lhs.shape[2]
    share = wsum.shape[3]
    piece = wsum.shape[4]
    chips = n_dom // 2
    pairs = width // PAIR
    blk = lax.axis_index("blk")
    dom = lax.axis_index("dom")
    chip = dom // 2
    core = dom - 2 * chip
    mate = dom + 1 - 2 * core

    def copy(src, dst, send, recv, target):
        return pltpu.make_async_remote_copy(
            src_ref=src,
            dst_ref=dst,
            send_sem=send,
            recv_sem=recv,
            device_id=target,
            device_id_type=MESH,
        )

    def each_peer(action):
        for j in range(n_blk):
            pl.when(blk != j)(functools.partial(action, j))

    barrier = pltpu.get_barrier_semaphore()
    steps = (-2, -1, 1, 2)

    def greet(target):
        pl.semaphore_signal(barrier, inc=1, device_id=target, device_id_type=MESH)

    each_peer(lambda j: greet({"blk": j}))
    for step in steps:
        there = (dom + step >= 0) & (dom + step < n_dom)
        pl.when(there)(functools.partial(lambda s: greet({"dom": dom + s}), step))

    x = x_ref[...].astype(F32)
    inverse = lax.rsqrt(jnp.mean(x * x, axis=-1, keepdims=True) + EPSILON)
    normed[...] = (x * inverse).astype(BF16)
    kv_s[:, :width] = mm(normed[...], wk_ref[...]).astype(BF16)
    kv_s[:, width:] = mm(normed[...], wv_ref[...]).astype(BF16)

    own_anchors = anchors.shape[1]
    anchor_count = n_blk * own_anchors
    spots = lax.broadcasted_iota(jnp.int32, (cells, BS), 0)
    for side in range(2):
        hits = jnp.where(spots == face_ref[side : side + 1, :], 1.0, 0.0)
        hot_s[:, side * BS : (side + 1) * BS] = hits.astype(BF16)
    turn = lax.broadcasted_iota(jnp.int32, (own_anchors, anchor_count), 1) % own_anchors
    same = lax.broadcasted_iota(jnp.int32, (own_anchors, anchor_count), 0) == turn
    listed = jnp.broadcast_to(anchor_ref[...].astype(F32), (8, own_anchors)).astype(BF16)
    repeated = mm(listed, jnp.where(same, 1.0, 0.0).astype(BF16))[:1]
    places = lax.broadcasted_iota(jnp.int32, (cells, anchor_count), 0).astype(F32)
    hot_s[:, 2 * BS :] = jnp.where(places == repeated, 1.0, 0.0).astype(BF16)
    picked = 2 * BS + anchors.shape[1]
    for part in range(2):
        columns = slice(part * width, (part + 1) * width)
        chosen = mm_tn(hot_s[:, : 3 * BS], kv_s[:, columns]).astype(BF16)
        faces[0, :, columns] = chosen[:BS]
        faces[1, :, columns] = chosen[BS : 2 * BS]
        anchors[blk, :, columns] = chosen[2 * BS : picked]

    expected = n_blk - 1
    for step in steps:
        there = (dom + step >= 0) & (dom + step < n_dom)
        expected = expected + jnp.where(there, 1, 0)
    pl.semaphore_wait(barrier, expected)

    has_low = dom > 0
    has_high = dom < n_dom - 1

    def anchor_copy(j):
        return copy(
            anchors.at[blk], anchors.at[blk], anc_send.at[j], anc_recv.at[blk], {"blk": j}
        )

    def anchor_arrival(j):
        return copy(anchors.at[j], anchors.at[j], anc_send.at[j], anc_recv.at[j], {"blk": j})

    def face_copy(side):
        step = 2 * side - 1
        return copy(
            faces.at[side],
            halo.at[1 - side],
            face_send.at[side],
            face_recv.at[1 - side],
            {"dom": dom + step},
        )

    def weight_of(j):
        return (j * rows) // width, (j * rows) % width

    def early_copy(j):
        weight, start = weight_of(j)
        if weight < 3:
            source, target = normed.at[:, start : start + rows], lhs.at[blk]
        else:
            source, target = dy_ref, rhs.at[blk]
        return copy(source, target, early_send.at[j], early_recv.at[blk], {"blk": j})

    def early_own(j):
        weight, start = weight_of(j)
        if weight < 3:
            lhs[j] = normed[:, start : start + rows]
        else:
            rhs[j] = dy_ref[...]

    def strip(h):
        return pl.ds(pl.multiple_of(h * PAIR, PAIR), PAIR)

    def late_copy(j, h):
        weight, start = weight_of(j)
        to = h - start // PAIR if weight == 3 else h
        source = grads.at[weight, :, strip(h)] if weight < 3 else att_b.at[:, strip(h)]
        target = rhs.at[blk, :, strip(to)] if weight < 3 else lhs.at[blk, :, strip(to)]
        return copy(source, target, late_send.at[j, to], late_recv.at[blk, to], {"blk": j})

    def send_late(weight, h):
        for j in range(n_blk):
            this, start = weight_of(j)
            if this != weight:
                continue

            def send(j=j):
                late_copy(j, h).start()

            def own(j=j, start=start):
                if weight < 3:
                    rhs[j, :, strip(h)] = grads[weight, :, strip(h)]
                else:
                    lhs[j, :, strip(h - start // PAIR)] = att_b[:, strip(h)]

            wanted = True
            if weight == 3 and rows < width:
                wanted = (h >= start // PAIR) & (h < (start + rows) // PAIR)
            pl.when((blk != j) & wanted)(send)
            pl.when((blk == j) & wanted)(own)

    def send_early(j):
        pl.when(blk != j)(lambda: early_copy(j).start())
        pl.when(blk == j)(lambda: early_own(j))

    each_peer(lambda j: anchor_copy(j).start())
    pl.when(has_low)(lambda: face_copy(0).start())
    pl.when(has_high)(lambda: face_copy(1).start())
    for j in range(n_blk):
        send_early(j)

    q_s[...] = mm(normed[...], wq_ref[...]).astype(BF16)
    g_s[...] = mm_nt(dy_ref[...], wo_ref[...]).astype(BF16)

    @pl.when(jnp.logical_not(has_low))
    def _():
        halo[0] = jnp.zeros(halo.shape[1:], BF16)
        hg_in[0] = jnp.zeros(hg_in.shape[1:], BF16)

    @pl.when(jnp.logical_not(has_high))
    def _():
        halo[1] = jnp.zeros(halo.shape[1:], BF16)
        hg_in[1] = jnp.zeros(hg_in.shape[1:], BF16)

    lane = lax.broadcasted_iota(jnp.int32, (1, PAIR), 1)
    first = jnp.where(lane < HEAD, 1.0, 0.0)
    first_b = first.astype(BF16)
    second_b = (1.0 - first).astype(BF16)

    def stacked(rows_of, scale):
        return jnp.concatenate([rows_of * (first_b * scale), rows_of * (second_b * scale)], 0)

    def unstacked(tensor):
        half = tensor.shape[0] // 2
        keep = jnp.broadcast_to(first, (half, PAIR)) > 0
        return jnp.where(keep, tensor[:half], tensor[half:])

    each_peer(lambda j: anchor_arrival(j).wait_recv())
    def anchor_pair(h, carry):
        sl = pl.ds(pl.multiple_of(h * PAIR, PAIR), PAIR)
        vsl = pl.ds(pl.multiple_of(width + h * PAIR, PAIR), PAIR)
        q2 = stacked(q_s[:, sl], SCALING)
        g2 = stacked(g_s[:, sl], 1.0)
        keys = anchors[:, :, sl].reshape(anchor_count, PAIR)
        values = anchors[:, :, vsl].reshape(anchor_count, PAIR)
        out, query_term, key_term, value_term = attend(q2, g2, keys, values, None)
        att_f[:, sl] = unstacked(out)
        qg_f[:, sl] = unstacked(query_term)
        ag_out[:, :, sl] = key_term.astype(BF16).reshape(n_blk, -1, PAIR)
        ag_out[:, :, vsl] = value_term.astype(BF16).reshape(n_blk, -1, PAIR)
        return carry

    lax.fori_loop(0, pairs, anchor_pair, 0)

    def ag_copy(j):
        return copy(ag_out.at[j], ag_in.at[blk], ag_send.at[j], ag_recv.at[blk], {"blk": j})

    def ag_arrival(j):
        return copy(ag_out.at[j], ag_in.at[j], ag_send.at[j], ag_recv.at[j], {"blk": j})

    each_peer(lambda j: ag_copy(j).start())
    ag_in[blk] = ag_out[blk]

    def face_arrival(side):
        step = 2 * side - 1
        return copy(
            faces.at[side],
            halo.at[side],
            face_send.at[side],
            face_recv.at[side],
            {"dom": dom + step},
        )

    pl.when(has_low)(lambda: face_arrival(0).wait_recv())
    pl.when(has_high)(lambda: face_arrival(1).wait_recv())

    blocks = cells // BS
    pool_rows = cells + 2 * BS
    spot = lax.broadcasted_iota(jnp.int32, (1, pool_rows), 1)
    zero = jnp.zeros((1, pool_rows), jnp.int32)
    one = zero + 1
    live_to = jnp.where(
        spot < cells, pool_rows, jnp.where(spot < cells + BS, cells, cells + BS)
    )
    live_to = live_to + jnp.where(
        spot < cells,
        0,
        jnp.where(spot < cells + BS, zero + count_ref[0, 0], zero + count_ref[0, 1]),
    )
    alive = jnp.where(spot < live_to, one, zero)
    live = []
    for j in range(blocks):
        listed = zero
        for i in range(near_ref.shape[1]):
            low = near_ref[j, i] * BS
            inside = jnp.where(spot >= low, one, zero) * jnp.where(spot < low + BS, one, zero)
            listed = listed + inside
        live.append((listed * alive).astype(F32))

    def hg_copy(side, h):
        step = 2 * side - 1
        return copy(
            hg_out.at[side, h],
            hg_in.at[1 - side, h],
            hg_send.at[side, h],
            hg_recv.at[1 - side, h],
            {"dom": dom + step},
        )

    def hg_arrival(side, h):
        step = 2 * side - 1
        return copy(
            hg_out.at[side, h],
            hg_in.at[side, h],
            hg_send.at[side, h],
            hg_recv.at[side, h],
            {"dom": dom + step},
        )

    def finish(h):
        pl.when(has_low)(lambda: hg_arrival(0, h).wait_recv())
        pl.when(has_high)(lambda: hg_arrival(1, h).wait_recv())
        sl = strip(h)
        vsl = pl.ds(pl.multiple_of(width + h * PAIR, PAIR), PAIR)
        shares = jnp.concatenate([ag_in[:, :, sl], ag_in[:, :, vsl]], -1)
        came = jnp.concatenate(
            [hg_in[0, h], hg_in[1, h], shares.reshape(anchor_count, 2 * PAIR)], 0
        )
        total = near_s[h] + mm(hot_s[...], came)
        grads[1, :, sl] = total[:, :PAIR].astype(BF16)
        grads[2, :, sl] = total[:, PAIR:].astype(BF16)
        send_late(1, h)
        send_late(2, h)

    def near_pair(h, carry):
        sl = pl.ds(pl.multiple_of(h * PAIR, PAIR), PAIR)
        vsl = pl.ds(pl.multiple_of(width + h * PAIR, PAIR), PAIR)
        keys = jnp.concatenate([kv_s[:, sl], halo[0, :, sl], halo[1, :, sl]], 0)
        values = jnp.concatenate([kv_s[:, vsl], halo[0, :, vsl], halo[1, :, vsl]], 0)
        key_sum = value_sum = None
        for j in range(blocks):
            own = slice(j * BS, (j + 1) * BS)
            q2 = stacked(q_s[own, sl], SCALING)
            g2 = stacked(g_s[own, sl], 1.0)
            out, query_term, key_term, value_term = attend(q2, g2, keys, values, live[j])
            att_b[own, sl] = (att_f[own, sl] + unstacked(out)).astype(BF16)
            grads[0, own, sl] = (qg_f[own, sl] + unstacked(query_term)).astype(BF16)
            key_sum = key_term if key_sum is None else key_sum + key_term
            value_sum = value_term if value_sum is None else value_sum + value_term
        near_s[h, :, :PAIR] = key_sum[:cells]
        near_s[h, :, PAIR:] = value_sum[:cells]
        for side in range(2):
            part = slice(cells + side * BS, cells + (side + 1) * BS)
            hg_out[side, h, :, :PAIR] = key_sum[part].astype(BF16)
            hg_out[side, h, :, PAIR:] = value_sum[part].astype(BF16)
        pl.when(has_low)(lambda: hg_copy(0, h).start())
        pl.when(has_high)(lambda: hg_copy(1, h).start())
        send_late(3, h)
        send_late(0, h)

        @pl.when(h == LAG)
        def _():
            each_peer(lambda j: ag_arrival(j).wait_recv())

        @pl.when(h >= LAG)
        def _():
            finish(h - LAG)

        return carry

    lax.fori_loop(0, pairs, near_pair, 0)

    for h in range(pairs - LAG, pairs):
        finish(h)
        if h == pairs - LAG:
            mixed = x_ref[...].astype(F32) + mm(att_b[...], wo_ref[...])
            mixed_ref[...] = mixed.astype(BF16)

    def cell_gradient():
        back = mm_nt(grads[0], wq_ref[...]) + mm_nt(grads[1], wk_ref[...])
        back = back + mm_nt(grads[2], wv_ref[...])
        x = x_ref[...].astype(F32)
        inverse = lax.rsqrt(jnp.mean(x * x, axis=-1, keepdims=True) + EPSILON)
        cube = inverse * inverse * inverse
        pull = jnp.mean(back * x, axis=-1, keepdims=True)
        total = dy_ref[...].astype(F32) + inverse * back - x * (cube * pull)
        cgrad_ref[...] = total.astype(BF16)

    is_out = blk * rows >= 3 * width

    def late_arrival(j, h, buffer):
        ref = buffer.at[j, :, strip(h)]
        return copy(ref, ref, late_send.at[j, h], late_recv.at[j, h], {"blk": j})

    def early_arrival(j, buffer):
        ref = buffer.at[j]
        return copy(ref, ref, early_send.at[j], early_recv.at[j], {"blk": j})

    def late_arrivals(buffer, low, high, j):
        def one(h, carry):
            late_arrival(j, h, buffer).wait_recv()
            return carry

        lax.fori_loop(low, high, one, 0)

    @pl.when(is_out)
    def _():
        each_peer(lambda j: early_arrival(j, rhs).wait_recv())
        each_peer(functools.partial(late_arrivals, lhs, 0, rows // PAIR))

    @pl.when(jnp.logical_not(is_out))
    def _():
        each_peer(lambda j: early_arrival(j, lhs).wait_recv())

    for j in range(n_blk):
        lhs_t[:, j * cells : (j + 1) * cells] = lhs[j].T

    def swap(n):
        return copy(
            wsum.at[n, 1 - core], wpart.at[n], core_send.at[n], core_recv.at[n], {"dom": mate}
        )

    strips = piece // PAIR

    def weight_piece(n):
        @pl.when(jnp.logical_not(is_out))
        def _():
            each_peer(functools.partial(late_arrivals, rhs, n * strips, (n + 1) * strips))

        columns = slice(n * piece, (n + 1) * piece)
        product = mm(lhs_t[...], rhs[:, :, columns].reshape(n_blk * cells, piece))
        for d in range(n_dom):
            wsum[n, d % 2, d // 2] = product[d * share : (d + 1) * share]
        swap(n).start()

    def right_copy(source, n, t):
        return copy(
            source.at[n, t],
            from_left.at[n, t],
            right_send.at[n, t],
            right_recv.at[n, t],
            {"dom": dom + 2},
        )

    def left_copy(source, n, t):
        return copy(
            source.at[n, t],
            from_right.at[n, t],
            left_send.at[n, t],
            left_recv.at[n, t],
            {"dom": dom - 2},
        )

    def right_arrival(n, t):
        ref = from_left.at[n, t]
        return copy(ref, ref, right_send.at[n, t], right_recv.at[n, t], {"dom": dom - 2})

    def left_arrival(n, t):
        ref = from_right.at[n, t]
        return copy(ref, ref, left_send.at[n, t], left_recv.at[n, t], {"dom": dom + 2})

    last = chips - 1

    def chain(n, step):
        t_right = last - step + chip
        t_left = step - (last - chip)
        if step == 0:
            swap(n).wait_recv()
            wpart[n] += wsum[n, core]

        @pl.when(chip == 0)
        def _():
            right_copy(wpart, n, t_right).start()

        @pl.when((chip > 0) & (chip <= step))
        def _():
            right_arrival(n, t_right).wait_recv()
            from_left[n, t_right] += wpart[n, t_right]
            right_copy(from_left, n, t_right).start()

        @pl.when(chip == last)
        def _():
            left_copy(wpart, n, t_left).start()

        @pl.when((chip < last) & (last - chip <= step))
        def _():
            left_arrival(n, t_left).wait_recv()
            from_right[n, t_left] += wpart[n, t_left]
            left_copy(from_right, n, t_left).start()

    for wave in range(PIECES + chips - 2):
        if wave < PIECES:
            weight_piece(wave)
        if wave == PIECES - 1:
            cell_gradient()
        for n in range(min(wave, PIECES - 1), -1, -1):
            if wave - n < chips - 1:
                chain(n, wave - n)

    for n in range(PIECES):
        columns = slice(n * piece, (n + 1) * piece)
        wgrad_ref[:, columns] = wpart[n, chip]

        @pl.when(chip > 0)
        def _():
            right_arrival(n, chip).wait_recv()
            wgrad_ref[:, columns] += from_left[n, chip]

        @pl.when(chip < last)
        def _():
            left_arrival(n, chip).wait_recv()
            wgrad_ref[:, columns] += from_right[n, chip]

    each_peer(lambda j: anchor_copy(j).wait_send())
    each_peer(lambda j: ag_copy(j).wait_send())
    each_peer(lambda j: early_copy(j).wait_send())

    def late_sent(j):
        weight, start = weight_of(j)
        low, high = (0, pairs) if weight < 3 else (start // PAIR, (start + rows) // PAIR)

        def one(h, carry):
            late_copy(j, h).wait_send()
            return carry

        lax.fori_loop(low, high, one, 0)

    each_peer(late_sent)

    def hg_sent(side):
        face_copy(side).wait_send()

        def one(h, carry):
            hg_copy(side, h).wait_send()
            return carry

        lax.fori_loop(0, pairs, one, 0)

    pl.when(has_low)(lambda: hg_sent(0))
    pl.when(has_high)(lambda: hg_sent(1))
    for n in range(PIECES):
        swap(n).wait_send()
        for step in range(chips - 1):
            t_right = last - step + chip
            t_left = step - (last - chip)

            @pl.when(chip <= step)
            def _():
                right_copy(from_left, n, t_right).wait_send()

            @pl.when(last - chip <= step)
            def _():
                left_copy(from_right, n, t_left).wait_send()


def deliver(*refs):
    count = len(refs) // 2
    for source, target in zip(refs[:count], refs[count:]):
        target[...] = source[...]


def body(
    cell_features,
    cotangent,
    query_weight,
    key_weight,
    value_weight,
    out_weight,
    anchor_index,
    face_cells,
    halo_count,
    neighbour_blocks,
):
    n_blk = lax.axis_size("blk")
    n_dom = lax.axis_size("dom")
    _, cells, width = cell_features.shape
    own_anchors = anchor_index.shape[1]
    rows = 4 * width // n_blk
    share = rows // n_dom
    chips = n_dom // 2
    piece = width // PIECES
    pairs = width // PAIR
    vmem = pl.BlockSpec(memory_space=pltpu.VMEM)
    smem = pl.BlockSpec(memory_space=pltpu.SMEM)
    dma = pltpu.SemaphoreType.DMA
    peers = [dma((n_blk,)) for _ in range(2)]
    sides = [dma((2,)) for _ in range(2)]
    chain = dma((PIECES, chips))
    mixed, cell_grad, weight_grads = pl.pallas_call(
        functools.partial(kernel, n_blk, n_dom),
        out_shape=(
            jax.ShapeDtypeStruct((cells, width), BF16),
            jax.ShapeDtypeStruct((cells, width), BF16),
            jax.ShapeDtypeStruct((share, width), F32),
        ),
        in_specs=[vmem] * 8 + [smem] * 2,
        out_specs=(vmem, vmem, vmem),
        scratch_shapes=[
            pltpu.VMEM((cells, width), BF16),
            pltpu.VMEM((cells, width), BF16),
            pltpu.VMEM((cells, width), BF16),
            pltpu.VMEM((cells, 2 * width), BF16),
            pltpu.VMEM((cells, 2 * BS + n_blk * own_anchors), BF16),
            pltpu.VMEM((2, BS, 2 * width), BF16),
            pltpu.VMEM((n_blk, own_anchors, 2 * width), BF16),
            pltpu.VMEM((2, BS, 2 * width), BF16),
            pltpu.VMEM((n_blk, own_anchors, 2 * width), BF16),
            pltpu.VMEM((n_blk, own_anchors, 2 * width), BF16),
            pltpu.VMEM((2, pairs, BS, 2 * PAIR), BF16),
            pltpu.VMEM((2, pairs, BS, 2 * PAIR), BF16),
            pltpu.VMEM((pairs, cells, 2 * PAIR), F32),
            pltpu.VMEM((cells, width), F32),
            pltpu.VMEM((cells, width), F32),
            pltpu.VMEM((cells, width), BF16),
            pltpu.VMEM((3, cells, width), BF16),
            pltpu.VMEM((n_blk, cells, rows), BF16),
            pltpu.VMEM((n_blk, cells, width), BF16),
            pltpu.VMEM((rows, n_blk * cells), BF16),
            pltpu.VMEM((PIECES, 2, chips, share, piece), F32),
            pltpu.VMEM((PIECES, chips, share, piece), F32),
            pltpu.VMEM((PIECES, chips, share, piece), F32),
            pltpu.VMEM((PIECES, chips, share, piece), F32),
            *peers,
            *sides,
            *peers,
            dma((n_blk, pairs)),
            dma((n_blk, pairs)),
            *peers,
            dma((2, pairs)),
            dma((2, pairs)),
            dma((PIECES,)),
            dma((PIECES,)),
            chain,
            chain,
            chain,
            chain,
        ],
        compiler_params=pltpu.CompilerParams(
            collective_id=0, has_side_effects=True, vmem_limit_bytes=56 * 1024 * 1024
        ),
    )(
        cell_features[0],
        cotangent[0],
        query_weight,
        key_weight,
        value_weight,
        out_weight,
        anchor_index,
        face_cells.reshape(2, BS),
        halo_count.reshape(1, 2),
        neighbour_blocks[0],
    )
    results = (mixed, cell_grad, weight_grads)
    mixed, cell_grad, weight_grads = pl.pallas_call(
        deliver,
        out_shape=tuple(jax.ShapeDtypeStruct(each.shape, each.dtype) for each in results),
        in_specs=[vmem] * 3,
        out_specs=(vmem,) * 3,
    )(*results)
    return mixed[None], cell_grad[None], weight_grads


def solution(mesh):
    return jax.shard_map(
        body,
        mesh=mesh,
        in_specs=(
            P("dom", "blk", None),
            P("dom", "blk", None),
            P(),
            P(),
            P(),
            P(),
            P("dom", "blk"),
            P("dom", "blk", None, None),
            P("dom", "blk", None),
            P("dom", "blk", None),
        ),
        out_specs=(P("dom", "blk", None), P("dom", "blk", None), P(("blk", "dom"), None)),
        check_vma=False,
    )
```

```python
import functools

import jax
import jax.numpy as jnp
from jax import lax
from jax.experimental import pallas as pl
from jax.experimental.pallas import tpu as pltpu
from jax.sharding import PartitionSpec as P

HEAD = 64
PAIR = 2 * HEAD
BS = 128
EPSILON = 1e-06
MASKED = -1e30
LAG = 3
PIECES = 3
SCALING = 0.125
MESH = pl.DeviceIdType.MESH
F32 = jnp.float32
BF16 = jnp.bfloat16


def mm(a, b):
    return lax.dot_general(a, b, (((1,), (0,)), ((), ())), preferred_element_type=F32)


def mm_nt(a, b):
    return lax.dot_general(a, b, (((1,), (1,)), ((), ())), preferred_element_type=F32)


def mm_tn(a, b):
    return lax.dot_general(a, b, (((0,), (0,)), ((), ())), preferred_element_type=F32)


def attend(q2, g2, keys, values, live):
    scores = mm_nt(q2, keys)
    if live is not None:
        scores = jnp.where(jnp.broadcast_to(live, scores.shape) > 0, scores, MASKED)
    powers = jnp.exp(scores - jnp.max(scores, axis=-1, keepdims=True))
    prob = powers * (1.0 / jnp.sum(powers, axis=-1, keepdims=True))
    prob_b = prob.astype(BF16)
    out = mm(prob_b, values)
    prob_grad = mm_nt(g2, values)
    score_grad = prob * (prob_grad - jnp.sum(prob * prob_grad, axis=-1, keepdims=True))
    score_b = score_grad.astype(BF16)
    query_term = mm(score_b, keys) * SCALING
    key_term = mm_tn(q2, score_b)
    value_term = mm_tn(g2, prob_b)
    return out, query_term, key_term, value_term


def kernel(
    n_blk,
    n_dom,
    x_ref,
    dy_ref,
    wq_ref,
    wk_ref,
    wv_ref,
    wo_ref,
    anchor_ref,
    face_ref,
    count_ref,
    near_ref,
    mixed_ref,
    cgrad_ref,
    wgrad_ref,
    normed,
    q_s,
    g_s,
    kv_s,
    hot_s,
    faces,
    anchors,
    halo,
    ag_out,
    ag_in,
    hg_out,
    hg_in,
    near_s,
    att_f,
    qg_f,
    att_b,
    grads,
    lhs,
    rhs,
    lhs_t,
    wsum,
    wpart,
    from_left,
    from_right,
    anc_send,
    anc_recv,
    face_send,
    face_recv,
    early_send,
    early_recv,
    late_send,
    late_recv,
    ag_send,
    ag_recv,
    hg_send,
    hg_recv,
    core_send,
    core_recv,
    right_send,
    right_recv,
    left_send,
    left_recv,
):
    cells, width = x_ref.shape
    rows = lhs.shape[2]
    share = wsum.shape[3]
    piece = wsum.shape[4]
    chips = n_dom // 2
    pairs = width // PAIR
    blk = lax.axis_index("blk")
    dom = lax.axis_index("dom")
    chip = dom // 2
    core = dom - 2 * chip
    mate = dom + 1 - 2 * core

    def copy(src, dst, send, recv, target):
        return pltpu.make_async_remote_copy(
            src_ref=src,
            dst_ref=dst,
            send_sem=send,
            recv_sem=recv,
            device_id=target,
            device_id_type=MESH,
        )

    def each_peer(action):
        for j in range(n_blk):
            pl.when(blk != j)(functools.partial(action, j))

    barrier = pltpu.get_barrier_semaphore()
    steps = (-2, -1, 1, 2)

    def greet(target):
        pl.semaphore_signal(barrier, inc=1, device_id=target, device_id_type=MESH)

    each_peer(lambda j: greet({"blk": j}))
    for step in steps:
        there = (dom + step >= 0) & (dom + step < n_dom)
        pl.when(there)(functools.partial(lambda s: greet({"dom": dom + s}), step))

    x = x_ref[...].astype(F32)
    inverse = lax.rsqrt(jnp.mean(x * x, axis=-1, keepdims=True) + EPSILON)
    normed[...] = (x * inverse).astype(BF16)
    kv_s[:, :width] = mm(normed[...], wk_ref[...]).astype(BF16)
    kv_s[:, width:] = mm(normed[...], wv_ref[...]).astype(BF16)

    own_anchors = anchors.shape[1]
    anchor_count = n_blk * own_anchors
    spots = lax.broadcasted_iota(jnp.int32, (cells, BS), 0)
    for side in range(2):
        hits = jnp.where(spots == face_ref[side : side + 1, :], 1.0, 0.0)
        hot_s[:, side * BS : (side + 1) * BS] = hits.astype(BF16)
    turn = lax.broadcasted_iota(jnp.int32, (own_anchors, anchor_count), 1) % own_anchors
    same = lax.broadcasted_iota(jnp.int32, (own_anchors, anchor_count), 0) == turn
    listed = jnp.broadcast_to(anchor_ref[...].astype(F32), (8, own_anchors)).astype(BF16)
    repeated = mm(listed, jnp.where(same, 1.0, 0.0).astype(BF16))[:1]
    places = lax.broadcasted_iota(jnp.int32, (cells, anchor_count), 0).astype(F32)
    hot_s[:, 2 * BS :] = jnp.where(places == repeated, 1.0, 0.0).astype(BF16)
    picked = 2 * BS + anchors.shape[1]
    for part in range(2):
        columns = slice(part * width, (part + 1) * width)
        chosen = mm_tn(hot_s[:, : 3 * BS], kv_s[:, columns]).astype(BF16)
        faces[0, :, columns] = chosen[:BS]
        faces[1, :, columns] = chosen[BS : 2 * BS]
        anchors[blk, :, columns] = chosen[2 * BS : picked]

    expected = n_blk - 1
    for step in steps:
        there = (dom + step >= 0) & (dom + step < n_dom)
        expected = expected + jnp.where(there, 1, 0)
    pl.semaphore_wait(barrier, expected)

    has_low = dom > 0
    has_high = dom < n_dom - 1

    def anchor_copy(j):
        return copy(
            anchors.at[blk], anchors.at[blk], anc_send.at[j], anc_recv.at[blk], {"blk": j}
        )

    def anchor_arrival(j):
        return copy(anchors.at[j], anchors.at[j], anc_send.at[j], anc_recv.at[j], {"blk": j})

    def face_copy(side):
        step = 2 * side - 1
        return copy(
            faces.at[side],
            halo.at[1 - side],
            face_send.at[side],
            face_recv.at[1 - side],
            {"dom": dom + step},
        )

    def weight_of(j):
        return (j * rows) // width, (j * rows) % width

    def early_copy(j):
        weight, start = weight_of(j)
        if weight < 3:
            source, target = normed.at[:, start : start + rows], lhs.at[blk]
        else:
            source, target = dy_ref, rhs.at[blk]
        return copy(source, target, early_send.at[j], early_recv.at[blk], {"blk": j})

    def early_own(j):
        weight, start = weight_of(j)
        if weight < 3:
            lhs[j] = normed[:, start : start + rows]
        else:
            rhs[j] = dy_ref[...]

    def strip(h):
        return pl.ds(pl.multiple_of(h * PAIR, PAIR), PAIR)

    def late_copy(j, h):
        weight, start = weight_of(j)
        to = h - start // PAIR if weight == 3 else h
        source = grads.at[weight, :, strip(h)] if weight < 3 else att_b.at[:, strip(h)]
        target = rhs.at[blk, :, strip(to)] if weight < 3 else lhs.at[blk, :, strip(to)]
        return copy(source, target, late_send.at[j, to], late_recv.at[blk, to], {"blk": j})

    def send_late(weight, h):
        for j in range(n_blk):
            this, start = weight_of(j)
            if this != weight:
                continue

            def send(j=j):
                late_copy(j, h).start()

            def own(j=j, start=start):
                if weight < 3:
                    rhs[j, :, strip(h)] = grads[weight, :, strip(h)]
                else:
                    lhs[j, :, strip(h - start // PAIR)] = att_b[:, strip(h)]

            wanted = True
            if weight == 3 and rows < width:
                wanted = (h >= start // PAIR) & (h < (start + rows) // PAIR)
            pl.when((blk != j) & wanted)(send)
            pl.when((blk == j) & wanted)(own)

    def send_early(j):
        pl.when(blk != j)(lambda: early_copy(j).start())
        pl.when(blk == j)(lambda: early_own(j))

    each_peer(lambda j: anchor_copy(j).start())
    pl.when(has_low)(lambda: face_copy(0).start())
    pl.when(has_high)(lambda: face_copy(1).start())
    for j in range(n_blk):
        send_early(j)

    q_s[...] = mm(normed[...], wq_ref[...]).astype(BF16)
    g_s[...] = mm_nt(dy_ref[...], wo_ref[...]).astype(BF16)

    @pl.when(jnp.logical_not(has_low))
    def _():
        halo[0] = jnp.zeros(halo.shape[1:], BF16)
        hg_in[0] = jnp.zeros(hg_in.shape[1:], BF16)

    @pl.when(jnp.logical_not(has_high))
    def _():
        halo[1] = jnp.zeros(halo.shape[1:], BF16)
        hg_in[1] = jnp.zeros(hg_in.shape[1:], BF16)

    lane = lax.broadcasted_iota(jnp.int32, (1, PAIR), 1)
    first = jnp.where(lane < HEAD, 1.0, 0.0)
    first_b = first.astype(BF16)
    second_b = (1.0 - first).astype(BF16)

    def stacked(rows_of, scale):
        return jnp.concatenate([rows_of * (first_b * scale), rows_of * (second_b * scale)], 0)

    def unstacked(tensor):
        half = tensor.shape[0] // 2
        keep = jnp.broadcast_to(first, (half, PAIR)) > 0
        return jnp.where(keep, tensor[:half], tensor[half:])

    each_peer(lambda j: anchor_arrival(j).wait_recv())
    def anchor_pair(h, carry):
        sl = pl.ds(pl.multiple_of(h * PAIR, PAIR), PAIR)
        vsl = pl.ds(pl.multiple_of(width + h * PAIR, PAIR), PAIR)
        q2 = stacked(q_s[:, sl], SCALING)
        g2 = stacked(g_s[:, sl], 1.0)
        keys = anchors[:, :, sl].reshape(anchor_count, PAIR)
        values = anchors[:, :, vsl].reshape(anchor_count, PAIR)
        out, query_term, key_term, value_term = attend(q2, g2, keys, values, None)
        att_f[:, sl] = unstacked(out)
        qg_f[:, sl] = unstacked(query_term)
        ag_out[:, :, sl] = key_term.T.astype(BF16).reshape(n_blk, -1, PAIR)
        ag_out[:, :, vsl] = value_term.T.astype(BF16).reshape(n_blk, -1, PAIR)
        return carry

    lax.fori_loop(0, pairs, anchor_pair, 0, unroll=2)

    def ag_copy(j):
        return copy(ag_out.at[j], ag_in.at[blk], ag_send.at[j], ag_recv.at[blk], {"blk": j})

    def ag_arrival(j):
        return copy(ag_out.at[j], ag_in.at[j], ag_send.at[j], ag_recv.at[j], {"blk": j})

    each_peer(lambda j: ag_copy(j).start())
    ag_in[blk] = ag_out[blk]

    def face_arrival(side):
        step = 2 * side - 1
        return copy(
            faces.at[side],
            halo.at[side],
            face_send.at[side],
            face_recv.at[side],
            {"dom": dom + step},
        )

    pl.when(has_low)(lambda: face_arrival(0).wait_recv())
    pl.when(has_high)(lambda: face_arrival(1).wait_recv())

    blocks = cells // BS
    pool_rows = cells + 2 * BS
    spot = lax.broadcasted_iota(jnp.int32, (1, pool_rows), 1)
    zero = jnp.zeros((1, pool_rows), jnp.int32)
    one = zero + 1
    live_to = jnp.where(
        spot < cells, pool_rows, jnp.where(spot < cells + BS, cells, cells + BS)
    )
    live_to = live_to + jnp.where(
        spot < cells,
        0,
        jnp.where(spot < cells + BS, zero + count_ref[0, 0], zero + count_ref[0, 1]),
    )
    alive = jnp.where(spot < live_to, one, zero)
    live = []
    for j in range(blocks):
        listed = zero
        for i in range(near_ref.shape[1]):
            low = near_ref[j, i] * BS
            inside = jnp.where(spot >= low, one, zero) * jnp.where(spot < low + BS, one, zero)
            listed = listed + inside
        live.append((listed * alive).astype(F32))

    def hg_copy(side, h):
        step = 2 * side - 1
        return copy(
            hg_out.at[side, h],
            hg_in.at[1 - side, h],
            hg_send.at[side, h],
            hg_recv.at[1 - side, h],
            {"dom": dom + step},
        )

    def hg_arrival(side, h):
        step = 2 * side - 1
        return copy(
            hg_out.at[side, h],
            hg_in.at[side, h],
            hg_send.at[side, h],
            hg_recv.at[side, h],
            {"dom": dom + step},
        )

    def finish(h):
        pl.when(has_low)(lambda: hg_arrival(0, h).wait_recv())
        pl.when(has_high)(lambda: hg_arrival(1, h).wait_recv())
        sl = strip(h)
        vsl = pl.ds(pl.multiple_of(width + h * PAIR, PAIR), PAIR)
        shares = jnp.concatenate([ag_in[:, :, sl], ag_in[:, :, vsl]], -1)
        came = jnp.concatenate(
            [hg_in[0, h], hg_in[1, h], shares.reshape(anchor_count, 2 * PAIR)], 0
        )
        total = near_s[h] + mm(hot_s[...], came)
        grads[1, :, sl] = total[:, :PAIR].astype(BF16)
        grads[2, :, sl] = total[:, PAIR:].astype(BF16)
        send_late(1, h)
        send_late(2, h)

    def near_pair(h, carry):
        sl = pl.ds(pl.multiple_of(h * PAIR, PAIR), PAIR)
        vsl = pl.ds(pl.multiple_of(width + h * PAIR, PAIR), PAIR)
        keys = jnp.concatenate([kv_s[:, sl], halo[0, :, sl], halo[1, :, sl]], 0)
        values = jnp.concatenate([kv_s[:, vsl], halo[0, :, vsl], halo[1, :, vsl]], 0)
        key_sum = value_sum = None
        for j in range(blocks):
            own = slice(j * BS, (j + 1) * BS)
            q2 = stacked(q_s[own, sl], SCALING)
            g2 = stacked(g_s[own, sl], 1.0)
            out, query_term, key_term, value_term = attend(q2, g2, keys, values, live[j])
            att_b[own, sl] = (att_f[own, sl] + unstacked(out)).astype(BF16)
            grads[0, own, sl] = (qg_f[own, sl] + unstacked(query_term)).astype(BF16)
            key_sum = key_term if key_sum is None else key_sum + key_term
            value_sum = value_term if value_sum is None else value_sum + value_term
        key_sum = key_sum.T
        value_sum = value_sum.T
        near_s[h, :, :PAIR] = key_sum[:cells]
        near_s[h, :, PAIR:] = value_sum[:cells]
        for side in range(2):
            part = slice(cells + side * BS, cells + (side + 1) * BS)
            hg_out[side, h, :, :PAIR] = key_sum[part].astype(BF16)
            hg_out[side, h, :, PAIR:] = value_sum[part].astype(BF16)
        pl.when(has_low)(lambda: hg_copy(0, h).start())
        pl.when(has_high)(lambda: hg_copy(1, h).start())
        send_late(3, h)
        send_late(0, h)

        @pl.when(h == LAG)
        def _():
            each_peer(lambda j: ag_arrival(j).wait_recv())

        @pl.when(h >= LAG)
        def _():
            finish(h - LAG)

        return carry

    lax.fori_loop(0, pairs, near_pair, 0)

    for h in range(pairs - LAG, pairs):
        finish(h)
        if h == pairs - LAG:
            mixed = x_ref[...].astype(F32) + mm(att_b[...], wo_ref[...])
            mixed_ref[...] = mixed.astype(BF16)

    def cell_gradient():
        back = mm_nt(grads[0], wq_ref[...]) + mm_nt(grads[1], wk_ref[...])
        back = back + mm_nt(grads[2], wv_ref[...])
        x = x_ref[...].astype(F32)
        inverse = lax.rsqrt(jnp.mean(x * x, axis=-1, keepdims=True) + EPSILON)
        cube = inverse * inverse * inverse
        pull = jnp.mean(back * x, axis=-1, keepdims=True)
        total = dy_ref[...].astype(F32) + inverse * back - x * (cube * pull)
        cgrad_ref[...] = total.astype(BF16)

    is_out = blk * rows >= 3 * width

    def late_arrival(j, h, buffer):
        ref = buffer.at[j, :, strip(h)]
        return copy(ref, ref, late_send.at[j, h], late_recv.at[j, h], {"blk": j})

    def early_arrival(j, buffer):
        ref = buffer.at[j]
        return copy(ref, ref, early_send.at[j], early_recv.at[j], {"blk": j})

    def late_arrivals(buffer, low, high, j):
        def one(h, carry):
            late_arrival(j, h, buffer).wait_recv()
            return carry

        lax.fori_loop(low, high, one, 0)

    @pl.when(is_out)
    def _():
        each_peer(lambda j: early_arrival(j, rhs).wait_recv())
        each_peer(functools.partial(late_arrivals, lhs, 0, rows // PAIR))

    @pl.when(jnp.logical_not(is_out))
    def _():
        each_peer(lambda j: early_arrival(j, lhs).wait_recv())

    for j in range(n_blk):
        lhs_t[:, j * cells : (j + 1) * cells] = lhs[j].T

    def swap(n):
        return copy(
            wsum.at[n, 1 - core], wpart.at[n], core_send.at[n], core_recv.at[n], {"dom": mate}
        )

    strips = piece // PAIR

    def weight_piece(n):
        @pl.when(jnp.logical_not(is_out))
        def _():
            each_peer(functools.partial(late_arrivals, rhs, n * strips, (n + 1) * strips))

        columns = slice(n * piece, (n + 1) * piece)
        product = mm(lhs_t[...], rhs[:, :, columns].reshape(n_blk * cells, piece))
        for d in range(n_dom):
            wsum[n, d % 2, d // 2] = product[d * share : (d + 1) * share]
        swap(n).start()

    def right_copy(source, n, t):
        return copy(
            source.at[n, t],
            from_left.at[n, t],
            right_send.at[n, t],
            right_recv.at[n, t],
            {"dom": dom + 2},
        )

    def left_copy(source, n, t):
        return copy(
            source.at[n, t],
            from_right.at[n, t],
            left_send.at[n, t],
            left_recv.at[n, t],
            {"dom": dom - 2},
        )

    def right_arrival(n, t):
        ref = from_left.at[n, t]
        return copy(ref, ref, right_send.at[n, t], right_recv.at[n, t], {"dom": dom - 2})

    def left_arrival(n, t):
        ref = from_right.at[n, t]
        return copy(ref, ref, left_send.at[n, t], left_recv.at[n, t], {"dom": dom + 2})

    last = chips - 1

    def chain(n, step):
        t_right = last - step + chip
        t_left = step - (last - chip)
        if step == 0:
            swap(n).wait_recv()
            wpart[n] += wsum[n, core]

        @pl.when(chip == 0)
        def _():
            right_copy(wpart, n, t_right).start()

        @pl.when((chip > 0) & (chip <= step))
        def _():
            right_arrival(n, t_right).wait_recv()
            from_left[n, t_right] += wpart[n, t_right]
            right_copy(from_left, n, t_right).start()

        @pl.when(chip == last)
        def _():
            left_copy(wpart, n, t_left).start()

        @pl.when((chip < last) & (last - chip <= step))
        def _():
            left_arrival(n, t_left).wait_recv()
            from_right[n, t_left] += wpart[n, t_left]
            left_copy(from_right, n, t_left).start()

    for wave in range(PIECES + chips - 2):
        if wave < PIECES:
            weight_piece(wave)
        if wave == PIECES - 1:
            cell_gradient()
        for n in range(min(wave, PIECES - 1), -1, -1):
            if wave - n < chips - 1:
                chain(n, wave - n)

    for n in range(PIECES):
        columns = slice(n * piece, (n + 1) * piece)
        wgrad_ref[:, columns] = wpart[n, chip]

        @pl.when(chip > 0)
        def _():
            right_arrival(n, chip).wait_recv()
            wgrad_ref[:, columns] += from_left[n, chip]

        @pl.when(chip < last)
        def _():
            left_arrival(n, chip).wait_recv()
            wgrad_ref[:, columns] += from_right[n, chip]

    each_peer(lambda j: anchor_copy(j).wait_send())
    each_peer(lambda j: ag_copy(j).wait_send())
    each_peer(lambda j: early_copy(j).wait_send())

    def late_sent(j):
        weight, start = weight_of(j)
        low, high = (0, pairs) if weight < 3 else (start // PAIR, (start + rows) // PAIR)

        def one(h, carry):
            late_copy(j, h).wait_send()
            return carry

        lax.fori_loop(low, high, one, 0)

    each_peer(late_sent)

    def hg_sent(side):
        face_copy(side).wait_send()

        def one(h, carry):
            hg_copy(side, h).wait_send()
            return carry

        lax.fori_loop(0, pairs, one, 0)

    pl.when(has_low)(lambda: hg_sent(0))
    pl.when(has_high)(lambda: hg_sent(1))
    for n in range(PIECES):
        swap(n).wait_send()
        for step in range(chips - 1):
            t_right = last - step + chip
            t_left = step - (last - chip)

            @pl.when(chip <= step)
            def _():
                right_copy(from_left, n, t_right).wait_send()

            @pl.when(last - chip <= step)
            def _():
                left_copy(from_right, n, t_left).wait_send()


def deliver(*refs):
    count = len(refs) // 2
    for source, target in zip(refs[:count], refs[count:]):
        target[...] = source[...]


def body(
    cell_features,
    cotangent,
    query_weight,
    key_weight,
    value_weight,
    out_weight,
    anchor_index,
    face_cells,
    halo_count,
    neighbour_blocks,
):
    n_blk = lax.axis_size("blk")
    n_dom = lax.axis_size("dom")
    _, cells, width = cell_features.shape
    own_anchors = anchor_index.shape[1]
    rows = 4 * width // n_blk
    share = rows // n_dom
    chips = n_dom // 2
    piece = width // PIECES
    pairs = width // PAIR
    vmem = pl.BlockSpec(memory_space=pltpu.VMEM)
    smem = pl.BlockSpec(memory_space=pltpu.SMEM)
    dma = pltpu.SemaphoreType.DMA
    peers = [dma((n_blk,)) for _ in range(2)]
    sides = [dma((2,)) for _ in range(2)]
    chain = dma((PIECES, chips))
    mixed, cell_grad, weight_grads = pl.pallas_call(
        functools.partial(kernel, n_blk, n_dom),
        out_shape=(
            jax.ShapeDtypeStruct((cells, width), BF16),
            jax.ShapeDtypeStruct((cells, width), BF16),
            jax.ShapeDtypeStruct((share, width), F32),
        ),
        in_specs=[vmem] * 8 + [smem] * 2,
        out_specs=(vmem, vmem, vmem),
        scratch_shapes=[
            pltpu.VMEM((cells, width), BF16),
            pltpu.VMEM((cells, width), BF16),
            pltpu.VMEM((cells, width), BF16),
            pltpu.VMEM((cells, 2 * width), BF16),
            pltpu.VMEM((cells, 2 * BS + n_blk * own_anchors), BF16),
            pltpu.VMEM((2, BS, 2 * width), BF16),
            pltpu.VMEM((n_blk, own_anchors, 2 * width), BF16),
            pltpu.VMEM((2, BS, 2 * width), BF16),
            pltpu.VMEM((n_blk, own_anchors, 2 * width), BF16),
            pltpu.VMEM((n_blk, own_anchors, 2 * width), BF16),
            pltpu.VMEM((2, pairs, BS, 2 * PAIR), BF16),
            pltpu.VMEM((2, pairs, BS, 2 * PAIR), BF16),
            pltpu.VMEM((pairs, cells, 2 * PAIR), F32),
            pltpu.VMEM((cells, width), F32),
            pltpu.VMEM((cells, width), F32),
            pltpu.VMEM((cells, width), BF16),
            pltpu.VMEM((3, cells, width), BF16),
            pltpu.VMEM((n_blk, cells, rows), BF16),
            pltpu.VMEM((n_blk, cells, width), BF16),
            pltpu.VMEM((rows, n_blk * cells), BF16),
            pltpu.VMEM((PIECES, 2, chips, share, piece), F32),
            pltpu.VMEM((PIECES, chips, share, piece), F32),
            pltpu.VMEM((PIECES, chips, share, piece), F32),
            pltpu.VMEM((PIECES, chips, share, piece), F32),
            *peers,
            *sides,
            *peers,
            dma((n_blk, pairs)),
            dma((n_blk, pairs)),
            *peers,
            dma((2, pairs)),
            dma((2, pairs)),
            dma((PIECES,)),
            dma((PIECES,)),
            chain,
            chain,
            chain,
            chain,
        ],
        compiler_params=pltpu.CompilerParams(
            collective_id=0, has_side_effects=True, vmem_limit_bytes=56 * 1024 * 1024
        ),
    )(
        cell_features[0],
        cotangent[0],
        query_weight,
        key_weight,
        value_weight,
        out_weight,
        anchor_index,
        face_cells.reshape(2, BS),
        halo_count.reshape(1, 2),
        neighbour_blocks[0],
    )
    results = (mixed, cell_grad, weight_grads)
    mixed, cell_grad, weight_grads = pl.pallas_call(
        deliver,
        out_shape=tuple(jax.ShapeDtypeStruct(each.shape, each.dtype) for each in results),
        in_specs=[vmem] * 3,
        out_specs=(vmem,) * 3,
    )(*results)
    return mixed[None], cell_grad[None], weight_grads


def solution(mesh):
    return jax.shard_map(
        body,
        mesh=mesh,
        in_specs=(
            P("dom", "blk", None),
            P("dom", "blk", None),
            P(),
            P(),
            P(),
            P(),
            P("dom", "blk"),
            P("dom", "blk", None, None),
            P("dom", "blk", None),
            P("dom", "blk", None),
        ),
        out_specs=(P("dom", "blk", None), P("dom", "blk", None), P(("blk", "dom"), None)),
        check_vma=False,
    )
```
